256 devices in a mesh: dp: 32 (over y, x, core), tensor: 8 (over z).
Axes of the slice: x: 4, y: 4, z: 8, core: 2. Of those that a mesh axis runs over, the one named last changes fastest.
Arguments:
- streams: bfloat16 [4, 8192, 5120], P(None, 'dp', 'tensor'), may hold values from -70 to 70
- stream_grads: bfloat16 [4, 8192, 5120], P(None, 'dp', 'tensor'), may hold values from -6 to 6
- branch_out: bfloat16 [8192, 5120], P('dp', 'tensor'), may hold values from -6 to 6
- query_grads: bfloat16 [8192, 5120], P('dp', 'tensor'), may hold values from -6 to 6
- query_weight: bfloat16 [5120, 5120], P(None, 'tensor'), may hold values from -0.078125 to 0.078125
- norm_gain: float32 [5120], P('tensor'), may hold values from 0.5 to 1.5
- coef_weight: bfloat16 [5120, 6], P('tensor'), may hold values from -0.078125 to 0.078125
- static_coef: float32 [4, 6], replicated, may hold values from -1 to 1
Outputs:
- streams_grad: bfloat16 [4, 8192, 5120], P(None, 'dp', 'tensor')
- branch_grad: bfloat16 [8192, 5120], P('dp', 'tensor')
- query_weight_grad: float32 [5120, 5120], P('dp', 'tensor')
- gain_grad: float32 [5120], P('tensor')
- coef_weight_grad: float32 [5120, 6], P('tensor')
- static_grad: float32 [4, 6], replicated
The draws below stay inside these ranges and needn't reach their ends.
All inputs are finite; a program needn't handle non-finite values.
Results may differ from the reference program's by a relative error of at most 0.0029.
Values may be sent and summed in bfloat16 or wider, within the bound.
A program may use at most 128 MiB of HBM per device.

```python
import math
import jax
import jax.numpy as jnp
from jax import lax

D = 5120
STREAMS = 4
E = 5120
COEFS = 6
TOKENS = 8192


def draw_streams(key, part):
    key = jax.random.fold_in(key, 11)
    key_list = jax.random.split(key, 3)
    column_pos = jnp.arange(D, dtype=jnp.float32) / max(D - 1, 1)
    ramp_scale = jnp.sqrt(1.0 + 2.0 * column_pos)
    col_scale = jnp.exp(jax.random.uniform(key_list[1], (D,), jnp.float32, 0.0, math.log(10.0)))
    row_scale = jnp.exp(jax.random.uniform(key_list[2], (STREAMS, TOKENS, 1), jnp.float32, 0.0, math.log(10.0)))
    base_vals = jnp.clip(jax.random.normal(key_list[0], (STREAMS, TOKENS, D), jnp.float32), -4.0, 4.0)
    return (base_vals * ramp_scale * col_scale * row_scale / 10.0).astype(jnp.bfloat16)


def block_scale(own_key, dims, cuts, low, high):
    factor_of, own = 1.0, jax.random.fold_in(own_key, 6)
    for axis_at, blocks in cuts:
        heights = jnp.exp(jax.random.uniform(jax.random.fold_in(own, axis_at), (blocks,), jnp.float32, low / len(cuts), high / len(cuts)))
        factor_of = factor_of * jnp.repeat(heights, dims[axis_at] // blocks).reshape([-1 if axis == axis_at else 1 for axis in range(len(dims))])
    return factor_of


def noise(key, dims, width, most, cuts=(), held_as=jnp.bfloat16):
    loudness = block_scale(key, dims, cuts, -0.22, 0.18) if cuts else 1.0
    values = jax.random.normal(key, dims, jnp.float32) * width * loudness
    return jnp.minimum(jnp.maximum(values, -most), most).astype(held_as)


def setup_inputs(seed: int = 0) -> dict:
    seeds = jax.random.split(jax.random.key(seed), 9)
    return {
        "streams": draw_streams(jax.random.fold_in(seeds[8], 71), 0),
        "stream_grads": noise(seeds[1], (STREAMS, TOKENS, D), 1.0, 6.0, ((1, 32), (2, 8))),
        "branch_out": noise(seeds[2], (TOKENS, D), 1.0, 6.0, ((0, 32), (1, 8))),
        "query_grads": noise(seeds[3], (TOKENS, E), 1.0, 6.0, ((0, 32), (1, 8))),
        "query_weight": noise(seeds[4], (D, E), D ** -0.5, 0.078125, ((1, 8),)),
        "norm_gain": jnp.clip(1.0 + 0.1 * jax.random.normal(seeds[5], (D,), jnp.float32), 0.5, 1.5),
        "coef_weight": noise(seeds[6], (D, COEFS), D ** -0.5, 0.078125, ((0, 8),)),
        "static_coef": jnp.clip(jax.random.uniform(seeds[7], (STREAMS, COEFS), jnp.float32, -1.0, 1.0), -1.0, 1.0),
    }


EPS = 1e-06
HIGH = lax.Precision.HIGHEST

def reference(streams, stream_grads, branch_out, query_grads, query_weight, norm_gain, coef_weight, static_coef):
    model_width = streams.shape[2]
    stream_vals = streams.astype(jnp.float32)
    grad_vals = stream_grads.astype(jnp.float32)
    branch_vals = branch_out.astype(jnp.float32)
    coef_w = coef_weight.astype(jnp.float32)
    sum_sq = jnp.einsum('itd,itd->ti', stream_vals, stream_vals, precision=HIGH)
    projected = jnp.einsum('itd,dc->tic', stream_vals, coef_w, precision=HIGH)
    inv_rms = lax.rsqrt(sum_sq / model_width + EPS)
    squashed = jnp.tanh(inv_rms[:, :, None] * projected)
    coeffs = static_coef[None] + squashed
    depth_coef = coeffs[:, :, 0]
    width_coef = coeffs[:, :, 1]
    route_coef = coeffs[:, :, 2:]
    mixed = jnp.einsum('ti,itd->td', width_coef, stream_vals, precision=HIGH)
    mix_inv = lax.rsqrt(lax.optimization_barrier(jnp.sum(mixed * mixed, axis=-1)) / model_width + EPS)
    normed = (mixed * mix_inv[:, None] * norm_gain[None]).astype(jnp.bfloat16)
    branch_grad = jnp.einsum('tj,jtd->td', depth_coef, grad_vals, precision=HIGH).astype(jnp.bfloat16)
    depth_grad = jnp.einsum('td,jtd->tj', branch_vals, grad_vals, precision=HIGH)
    route_grad = jnp.einsum('itd,jtd->tij', stream_vals, grad_vals, precision=HIGH)
    direct = jnp.einsum('tij,jtd->itd', route_coef, grad_vals, precision=HIGH)
    norm_grad = jnp.dot(query_grads, query_weight.T, preferred_element_type=jnp.float32)
    weight_grad = jnp.dot(normed.T, query_grads, preferred_element_type=jnp.float32)
    gain_grad = lax.optimization_barrier(jnp.sum(norm_grad * mixed * mix_inv[:, None], axis=0))
    scaled_grad = norm_grad * norm_gain[None]
    inner_sum = lax.optimization_barrier(jnp.sum(scaled_grad * mixed, axis=-1))
    mixed_grad = mix_inv[:, None] * scaled_grad - mixed * (mix_inv ** 3 * inner_sum / model_width)[:, None]
    mix_grad = jnp.einsum('itd,td->ti', stream_vals, mixed_grad, precision=HIGH)
    coef_grad = jnp.concatenate([depth_grad[:, :, None], mix_grad[:, :, None], route_grad], axis=-1)
    pre_grad = coef_grad * (1.0 - squashed * squashed)
    proj_grad = pre_grad * inv_rms[:, :, None]
    scale_grad = lax.optimization_barrier(jnp.sum(pre_grad * projected, axis=-1))
    coef_wgrad = jnp.einsum('itd,tic->dc', stream_vals, proj_grad, precision=HIGH)
    static_grad = lax.optimization_barrier(jnp.sum(coef_grad, axis=0))
    stream_out = direct + width_coef.T[:, :, None] * mixed_grad[None]
    stream_out = stream_out + jnp.einsum('tic,dc->itd', proj_grad, coef_w, precision=HIGH)
    stream_out = stream_out - (scale_grad * inv_rms ** 3 / model_width).T[:, :, None] * stream_vals
    return (stream_out.astype(jnp.bfloat16), branch_grad, weight_grad, gain_grad, coef_wgrad, static_grad)
```

```python
import functools

import jax
import jax.numpy as jnp
from jax import lax
from jax.experimental import pallas as pl
from jax.experimental.pallas import tpu as pltpu
from jax.sharding import PartitionSpec as P

EPS = 1e-06
MESH = pl.DeviceIdType.MESH
F32 = jnp.float32
BF16 = jnp.bfloat16

T = 256
F = 640
NZ = 8
D = F * NZ
RB = 160
HB = RB // 2
NX = 4
NY = 4


def dot_nt(a, b):
    return lax.dot_general(a, b, (((1,), (1,)), ((), ())), preferred_element_type=F32)


def dot_nn(a, b):
    return lax.dot_general(a, b, (((1,), (0,)), ((), ())), preferred_element_type=F32)


def split3(v):
    hi = v.astype(BF16).astype(F32)
    rest = v - hi
    mid = rest.astype(BF16).astype(F32)
    return hi, mid, (rest - mid).astype(BF16).astype(F32)


def kernel(
    s_h, g_h, b_h, q_h, w_h, gain, cw, st,
    so_h, bo_h, wo_h, gain_o, cw_o, st_o,
    xs, gs, qq, wbuf,
    pbuf, rs_send, rs_recv,
    cl, r1, cfull, hbuf,
    mixed, nts, nbuf, col1, col2, cwx,
    xsend, xrecv, keep, xa, wo_v,
    so_v, bo_v, acc, sb, sc, sx, sy,
    in_sem, win_sem, out_sem,
    rs_ss, rs_rs, ag_ss, ag_rs, sync_ss, sync_rs, core_ss, core_rs, x_ss, x_rs, sm_ss, sm_rs,
):
    dp = lax.axis_index("dp")
    z = lax.axis_index("tensor")
    core = lax.rem(dp, 2)
    x = lax.rem(dp // 2, NX)
    y = dp // (2 * NX)

    def zdev(k):
        return (dp, lax.rem(z + k + NZ, NZ))

    def xdev(k):
        return ((y * NX + lax.rem(x + k + NX, NX)) * 2 + core, z)

    def ydev(k):
        return ((lax.rem(y + k + NY, NY) * NX + x) * 2 + core, z)

    cdev = (dp + 1 - 2 * core, z)

    def rcopy(src, dst, ss, rs, dev):
        return pltpu.make_async_remote_copy(
            src_ref=src, dst_ref=dst, send_sem=ss, recv_sem=rs, device_id=dev, device_id_type=MESH
        )

    q_in = pltpu.make_async_copy(q_h, qq.at[core], in_sem.at[0])
    s_in = pltpu.make_async_copy(s_h, xs.at[0:4], in_sem.at[1])
    g_in = pltpu.make_async_copy(g_h, gs, in_sem.at[2])
    b_in = pltpu.make_async_copy(b_h, xs.at[4], in_sem.at[3])

    def w_in(k):
        blk = lax.rem(z + k, NZ)
        return pltpu.make_async_copy(
            w_h.at[pl.ds(pl.multiple_of(blk * F, F), F)], wbuf.at[k], win_sem.at[k]
        )

    q_in.start()
    w_in(4).start()
    s_in.start()
    g_in.start()
    b_in.start()
    for k in (3, 5, 2, 6, 1, 7, 0):
        w_in(k).start()

    barrier = pltpu.get_barrier_semaphore()
    peers = [zdev(k) for k in range(1, NZ)] + [xdev(k) for k in (1, 2, 3)]
    peers += [ydev(k) for k in (1, 2, 3)] + [cdev]
    for dev in peers:
        pl.semaphore_signal(barrier, inc=1, device_id=dev, device_id_type=MESH)

    def rs_partial(k):
        w_in(k).wait()
        pbuf[k] = dot_nt(qq[core], wbuf[k])

    RIGHT, LEFT = 0, 1
    HALF = T // 2

    def rs_copy(way, step, half):
        return rcopy(
            rs_send.at[way, step, half],
            rs_recv.at[way, step, half],
            rs_ss.at[way, step, half],
            rs_rs.at[way, step, half],
            zdev(1 if way == RIGHT else -1),
        )

    def rs_block(way, step):
        return 4 - step if way == RIGHT else 4 + step if step else 4

    def rs_raw(way, step, half):
        rs_send[way, step, half] = pbuf[rs_block(way, step), half * HALF : (half + 1) * HALF].astype(BF16)
        rs_copy(way, step, half).start()

    def rs_add(way, step, half):
        rs_copy(way, step - 1, half).wait_recv()
        v = pbuf[rs_block(way, step), half * HALF : (half + 1) * HALF]
        rs_send[way, step, half] = (v + rs_recv[way, step - 1, half].astype(F32)).astype(BF16)
        rs_copy(way, step, half).start()

    q_in.wait()
    rs_partial(4)
    pl.semaphore_wait(barrier, len(peers))
    rs_raw(RIGHT, 0, 0)
    rs_raw(LEFT, 0, 1)
    q_swap = rcopy(qq.at[core], qq.at[core], core_ss.at[0], core_rs.at[0], cdev)
    q_swap.start()
    rs_partial(3)
    rs_raw(RIGHT, 1, 1)
    rs_partial(5)
    rs_raw(LEFT, 1, 0)

    s_in.wait()
    g_in.wait()
    b_in.wait()
    cw8 = jnp.concatenate([cw[...].astype(F32), jnp.zeros((10, F), F32)], axis=0).astype(BF16)
    rows_i = lax.broadcasted_iota(jnp.int32, (128, 128), 0)
    cols_i = lax.broadcasted_iota(jnp.int32, (128, 128), 1)
    eye = rows_i == cols_i

    def diag(block):
        return jnp.sum(jnp.where(eye, block, 0.0), axis=0, keepdims=True)

    def gram(blk, carry):
        at = pl.ds(pl.multiple_of(blk * 128, 128), 128)
        sb_blk = xs[:, at, :].reshape(5 * 128, F)
        g_blk = gs[:, at, :].reshape(4 * 128, F)
        sg = dot_nt(sb_blk, g_blk)
        route = [
            [diag(sg[i * 128 : i * 128 + 128, j * 128 : j * 128 + 128]) for j in range(4)] for i in range(5)
        ]
        s_blk = sb_blk[: 4 * 128]
        ss = dot_nt(s_blk, s_blk)
        gr = {
            (i, j): diag(ss[i * 128 : i * 128 + 128, j * 128 : j * 128 + 128])
            for i in range(4)
            for j in range(i, 4)
        }
        proj = dot_nt(cw8, s_blk)
        zero = jnp.zeros((1, 128), F32)
        for i in range(4):
            cl[i, :, at] = jnp.concatenate(
                [proj[0:6, i * 128 : i * 128 + 128], gr[i, i], route[4][i]], axis=0
            )
        for half in range(2):
            cl[4 + half, :, at] = jnp.concatenate(
                [route[2 * half + i][j] for i in range(2) for j in range(4)], axis=0
            )
        cl[6, :, at] = jnp.concatenate(
            [gr[0, 1], gr[0, 2], gr[0, 3], gr[1, 2], gr[1, 3], gr[2, 3], zero, zero], axis=0
        )
        cl[7, :, at] = jnp.zeros((8, 128), F32)
        return carry

    lax.fori_loop(0, 2, gram, 0)

    def sync_out(k):
        return rcopy(
            cl.at[lax.rem(z + k, NZ)], r1.at[k], sync_ss.at[0, k], sync_rs.at[0, k], zdev(k)
        )

    def sync_back(k):
        return rcopy(cfull.at[z], cfull.at[z], sync_ss.at[1, k], sync_rs.at[1, k], zdev(k))

    def sync_back_in(k):
        at = cfull.at[lax.rem(z - k + NZ, NZ)]
        return rcopy(at, at, sync_ss.at[1, k], sync_rs.at[1, k], zdev(k))

    for k in range(1, NZ):
        sync_out(k).start()

    rs_partial(2)
    rs_partial(6)
    rs_add(RIGHT, 1, 0)
    rs_add(LEFT, 1, 1)

    total = cl[z]
    for k in range(1, NZ):
        sync_out(k).wait_recv()
        total = total + r1[k]
    cfull[z] = total
    for k in range(1, NZ):
        sync_back(k).start()

    rs_add(RIGHT, 2, 1)
    rs_add(LEFT, 2, 0)
    rs_partial(1)
    rs_partial(7)
    rs_partial(0)

    cw_f = cw8[0:8].astype(F32)
    for i in range(4):
        parts = [cw_f, cw_f, cw_f]
        if i:
            parts = [jnp.zeros((i * 32, F), F32)] + parts
        parts = parts + [jnp.zeros((128 - i * 32 - 24, F), F32)]
        cwx[i] = jnp.concatenate(parts, axis=0).astype(BF16)

    for k in range(1, NZ):
        sync_back_in(k).wait_recv()

    row8 = lax.broadcasted_iota(jnp.int32, (8, T), 0)

    def coefficients():
        proj, inv, sq, cf = [], [], [], []
        for i in range(4):
            piece = cfull[i]
            p8 = jnp.where(row8 < 6, piece, 0.0)
            iv = lax.rsqrt(piece[6:7] / D + EPS)
            th = jnp.tanh(iv * p8)
            stc = jnp.zeros((8, T), F32)
            for c in range(6):
                stc = jnp.where(row8 == c, st[i, c], stc)
            proj.append(p8)
            inv.append(iv)
            sq.append(th)
            cf.append(stc + th)
        off = cfull[6]
        at = {(0, 1): 0, (0, 2): 1, (0, 3): 2, (1, 2): 3, (1, 3): 4, (2, 3): 5}

        def g_of(i, j):
            if i == j:
                return cfull[i][6:7]
            r = at[min(i, j), max(i, j)]
            return off[r : r + 1]

        wid = [cf[i][1:2] for i in range(4)]
        gw = [sum(g_of(i, j) * wid[j] for j in range(4)) for i in range(4)]
        mixed_sq = sum(wid[i] * gw[i] for i in range(4))
        mix_inv = lax.rsqrt(mixed_sq / D + EPS)
        return proj, inv, sq, cf, wid, gw, mix_inv

    _, _, _, cf, _, _, mix_inv = coefficients()
    rows = jnp.concatenate(cf + [jnp.broadcast_to(mix_inv, (8, T)), jnp.zeros((88, T), F32)], axis=0)
    col1[...] = rows.T

    def mix(blk, carry):
        at = pl.ds(pl.multiple_of(blk * 32, 32), 32)
        c = col1[at, :]
        m = c[:, 1:2] * xs[0, at, :].astype(F32)
        for i in range(1, 4):
            m = m + c[:, 8 * i + 1 : 8 * i + 2] * xs[i, at, :].astype(F32)
        mixed[at, :] = m
        acc[0, at, :] = m * c[:, 32:33] * gain[...]
        return carry

    lax.fori_loop(0, T // 32, mix, 0)
    for k in range(4):
        pass
    for lane in range(F // 128):
        tr = acc[0, :, lane * 128 : lane * 128 + 128].T.astype(BF16)
        nts[lane * 128 : lane * 128 + 128, :] = tr

    def n_swap(kk):
        return rcopy(
            nts.at[pl.ds(pl.multiple_of((2 * kk + 1 - core) * RB, 32), RB)],
            nbuf.at[z, kk, core],
            core_ss.at[1 + kk],
            core_rs.at[1 + kk],
            cdev,
        )

    def n_swap_in(kk):
        return rcopy(
            nts.at[pl.ds(pl.multiple_of((2 * kk + 1 - core) * RB, 32), RB)],
            nbuf.at[z, kk, 1 - core],
            core_ss.at[1 + kk],
            core_rs.at[1 + kk],
            cdev,
        )

    for kk in range(2):
        n_swap(kk).start()
    for kk in range(2):
        nbuf[z, kk, core] = nts[pl.ds(pl.multiple_of((2 * kk + core) * RB, 32), RB), :]

    rs_add(RIGHT, 2, 0)
    rs_add(LEFT, 2, 1)

    def ag_copy(way, step, kk):
        blk = lax.rem(z - step + 1 + NZ, NZ) if way == RIGHT else lax.rem(z + step - 1, NZ)
        at = nbuf.at[blk, kk]
        return rcopy(at, at, ag_ss.at[way, step, kk], ag_rs.at[way, step, kk], zdev(1 if way == RIGHT else -1))

    def ag_in(way, step, kk):
        blk = lax.rem(z - step + NZ, NZ) if way == RIGHT else lax.rem(z + step, NZ)
        at = nbuf.at[blk, kk]
        return rcopy(at, at, ag_ss.at[way, step, kk], ag_rs.at[way, step, kk], zdev(1 if way == RIGHT else -1))

    for kk in range(2):
        n_swap_in(kk).wait_recv()
        ag_copy(RIGHT, 1, kk).start()
        ag_copy(LEFT, 1, kk).start()

    def ag_forward(step):
        for kk in range(2):
            for way in (RIGHT, LEFT):
                ag_in(way, step - 1, kk).wait_recv()
                if step < 4 or kk == way:
                    ag_copy(way, step, kk).start()

    par = lax.rem(z, 2)
    z0 = z - par
    q_swap_in = rcopy(qq.at[1 - core], qq.at[1 - core], core_ss.at[0], core_rs.at[0], cdev)
    q_swap_in.wait_recv()

    def pair_base(m):
        if m == 0:
            return z0
        if m == 3:
            return lax.rem(z0 + 4, NZ)
        sign = -1 if m == 1 else 1
        return lax.rem(z0 + sign * 2 * (1 - 2 * par) + NZ, NZ)

    def wg_block(m, r):
        xd = lax.rem(x + r, NX)
        n = nbuf.at[lax.rem(pair_base(m) + xd // 2, NZ), lax.rem(xd, 2)]
        return dot_nn(n[0], qq[0]) + dot_nn(n[1], qq[1])

    def red_copy(e, way, part):
        dev = (xdev if e < 4 else ydev)(1 if way == RIGHT else -1)
        return rcopy(
            xsend.at[e, way, part], xrecv.at[e, way, part], x_ss.at[e, way, part], x_rs.at[e, way, part], dev
        )

    def red_start(e, block):
        far = block(2).astype(BF16)
        xsend[e, RIGHT, 0] = far[:HB]
        red_copy(e, RIGHT, 0).start()
        xsend[e, LEFT, 0] = far[HB:]
        red_copy(e, LEFT, 0).start()
        near = block(1)
        xsend[e, RIGHT, 1] = near[HB:].astype(BF16)
        red_copy(e, RIGHT, 1).start()
        keep[e, RIGHT] = near[:HB]
        near = block(3)
        xsend[e, LEFT, 1] = near[:HB].astype(BF16)
        red_copy(e, LEFT, 1).start()
        keep[e, LEFT] = near[HB:]

    def red_forward(e):
        for way in (RIGHT, LEFT):
            red_copy(e, way, 0).wait_recv()
            xsend[e, way, 2] = (keep[e, way] + xrecv[e, way, 0].astype(F32)).astype(BF16)
            red_copy(e, way, 2).start()

    def red_finish(e, own):
        for way in (RIGHT, LEFT):
            for part in (1, 2):
                red_copy(e, way, part).wait_recv()
        top = own[:HB] + xrecv[e, RIGHT, 2].astype(F32) + xrecv[e, LEFT, 1].astype(F32)
        low = own[HB:] + xrecv[e, RIGHT, 1].astype(F32) + xrecv[e, LEFT, 2].astype(F32)
        return top, low

    def pair_start(m):
        red_start(m, functools.partial(wg_block, m))
        xa[pair_base(m) // 2] = wg_block(m, 0)

    def pair_finish(m):
        at = pair_base(m) // 2
        top, low = red_finish(m, xa[at])
        xa[at, :HB] = top
        xa[at, HB:] = low

    def branch(blk, carry):
        at = pl.ds(pl.multiple_of(blk * 32, 32), 32)
        c = col1[at, :]
        v = c[:, 0:1] * gs[0, at, :].astype(F32)
        for j in range(1, 4):
            v = v + c[:, 8 * j : 8 * j + 1] * gs[j, at, :].astype(F32)
        bo_v[at, :] = v.astype(BF16)
        return carry

    rs_add(RIGHT, 3, 1)
    rs_add(LEFT, 3, 0)
    lax.fori_loop(0, T // 32, branch, 0)
    bo_out = pltpu.make_async_copy(bo_v, bo_h, out_sem.at[0])
    bo_out.start()
    rs_add(RIGHT, 3, 0)
    rs_add(LEFT, 3, 1)

    ag_forward(2)
    pair_start(0)

    for way in (RIGHT, LEFT):
        for half in range(2):
            rs_copy(way, 3, half).wait_recv()

    def norm(blk, gain_sum):
        at = pl.ds(pl.multiple_of(blk * 128, 128), 128)
        ng = pbuf[0, at, :] + rs_recv[RIGHT, 3, blk].astype(F32) + rs_recv[LEFT, 3, blk].astype(F32)
        gain_sum = gain_sum + jnp.sum(ng * (mixed[at, :] * col1[at, 32:33]), axis=0, keepdims=True)
        scaled = ng * gain[...]
        pbuf[0, at, :] = scaled
        hi, mid, lo = split3(scaled)
        parts = jnp.concatenate([hi, mid, lo], axis=0).astype(BF16)
        prod = dot_nt(xs[0:4, at, :].reshape(4 * 128, F), parts)
        h = []
        for i in range(4):
            p = prod[i * 128 : i * 128 + 128]
            h.append(diag(p[:, 0:128] + p[:, 128:256] + p[:, 256:384]))
        hbuf[z, :, at] = jnp.concatenate(h + [jnp.zeros((4, 128), F32)], axis=0)
        return gain_sum

    gain_part = lax.fori_loop(0, T // 128, norm, jnp.zeros((1, F), F32))

    def h_out(k):
        return rcopy(hbuf.at[z], hbuf.at[z], sync_ss.at[2, k], sync_rs.at[2, k], zdev(k))

    def h_in(k):
        at = hbuf.at[lax.rem(z - k + NZ, NZ)]
        return rcopy(at, at, sync_ss.at[2, k], sync_rs.at[2, k], zdev(k))

    for k in range(1, NZ):
        h_out(k).start()

    red_forward(0)
    ag_forward(3)
    pair_start(1)

    for k in range(1, NZ):
        h_in(k).wait_recv()

    proj, inv, sq, cf, wid, gw, mix_inv = coefficients()
    h8 = hbuf[0]
    for k in range(1, NZ):
        h8 = h8 + hbuf[k]
    inner = sum(wid[i] * h8[i : i + 1] for i in range(4))
    kfac = mix_inv * mix_inv * mix_inv * inner / D
    rows, left, stat = [], [], []
    for i in range(4):
        mix_grad = mix_inv * h8[i : i + 1] - kfac * gw[i]
        route = cfull[4 + i // 2][4 * (i % 2) : 4 * (i % 2) + 4]
        cg = jnp.concatenate([cfull[i][7:8], mix_grad, route, jnp.zeros((2, T), F32)], axis=0)
        pre = cg * (1.0 - sq[i] * sq[i])
        pg = pre * inv[i]
        scale = jnp.sum(pre * proj[i], axis=0, keepdims=True) * (inv[i] * inv[i] * inv[i] / D)
        hi, mid, lo = split3(pg)
        left.append(jnp.concatenate([hi, mid, lo], axis=0))
        rows += [hi, mid, lo, wid[i], scale, cf[i][2:6], mix_inv, kfac]
        stat.append(jnp.broadcast_to(jnp.sum(cg, axis=1, keepdims=True), (8, 128)))
    col2[...] = jnp.concatenate(rows, axis=0).T
    cpart = dot_nn(jnp.concatenate(left, axis=1).astype(BF16), xs[0:4].reshape(4 * T, F))
    cpart = cpart[0:8] + cpart[8:16] + cpart[16:24]
    sb[0:8, :] = jnp.concatenate([cpart[0:6], gain_part, jnp.zeros((1, F), F32)], axis=0)
    sb[8:16, :] = jnp.concatenate(stat + [jnp.zeros((8, 128), F32)], axis=1)

    sm_core = rcopy(sb, sc, sm_ss.at[0], sm_rs.at[0], cdev)
    sm_core.start()

    lhs = col2[...].astype(BF16)
    for i in range(4):
        acc[i] = dot_nn(lhs, cwx[i])

    def out_rows(blk, carry):
        at = pl.ds(pl.multiple_of(blk * 16, 16), 16)
        c = col2[at, :]
        mg = c[:, 30:31] * pbuf[0, at, :] - c[:, 31:32] * mixed[at, :]
        g = [gs[j, at, :].astype(F32) for j in range(4)]
        for i in range(4):
            o = 32 * i + 24
            v = acc[i, at, :] + c[:, o : o + 1] * mg - c[:, o + 1 : o + 2] * xs[i, at, :].astype(F32)
            for j in range(4):
                v = v + c[:, o + 2 + j : o + 3 + j] * g[j]
            so_v[i, at, :] = v.astype(BF16)
        return carry

    ag_forward(4)
    lax.fori_loop(0, T // 16, out_rows, 0)
    so_out = pltpu.make_async_copy(so_v, so_h, out_sem.at[1])
    so_out.start()

    red_forward(1)
    pair_start(2)

    def sm_x(k):
        return rcopy(sx.at[x], sx.at[x], sm_ss.at[k], sm_rs.at[k], xdev(k))

    def sm_x_in(k):
        at = sx.at[lax.rem(x - k + NX, NX)]
        return rcopy(at, at, sm_ss.at[k], sm_rs.at[k], xdev(k))

    def sm_y(k):
        return rcopy(sy.at[y], sy.at[y], sm_ss.at[3 + k], sm_rs.at[3 + k], ydev(k))

    def sm_y_in(k):
        at = sy.at[lax.rem(y - k + NY, NY)]
        return rcopy(at, at, sm_ss.at[3 + k], sm_rs.at[3 + k], ydev(k))

    sm_core.wait_recv()
    sx[x] = sb[...] + sc[...]
    for k in (1, 2, 3):
        sm_x(k).start()

    ag_in(RIGHT, 4, 0).wait_recv()
    ag_in(LEFT, 4, 1).wait_recv()
    pair_start(3)
    red_forward(2)
    red_forward(3)

    for k in (1, 2, 3):
        sm_x_in(k).wait_recv()
    sy[y] = sx[0] + sx[1] + sx[2] + sx[3]
    for k in (1, 2, 3):
        sm_y(k).start()

    for m in range(4):
        pair_finish(m)

    red_start(4, lambda r: xa[lax.rem(y + r, NY)])
    for k in (1, 2, 3):
        sm_y_in(k).wait_recv()
    small = sy[0] + sy[1] + sy[2] + sy[3]
    cw_o[...] = small[0:6]
    gain_o[...] = small[6:7]
    lane = lax.broadcasted_iota(jnp.int32, (8, 128), 1)
    st8 = jnp.zeros((8, 128), F32)
    for i in range(4):
        st8 = jnp.where(lane == i, small[8:16, i * 128 : i * 128 + 128], st8)
    st_o[...] = st8
    red_forward(4)
    top, low = red_finish(4, xa[y])
    wo_v[:HB] = top
    wo_v[HB:] = low
    wo_out = pltpu.make_async_copy(wo_v, wo_h, out_sem.at[2])
    wo_out.start()

    for way in (RIGHT, LEFT):
        for step in range(4):
            for half in range(2):
                if step or half == way:
                    rs_copy(way, step, half).wait_send()
        for step in range(1, 5):
            for kk in range(2):
                if step < 4 or kk == way:
                    ag_copy(way, step, kk).wait_send()
        for e in range(5):
            for part in range(3):
                red_copy(e, way, part).wait_send()
    for k in range(1, NZ):
        sync_out(k).wait_send()
        sync_back(k).wait_send()
        h_out(k).wait_send()
    q_swap.wait_send()
    for kk in range(2):
        n_swap(kk).wait_send()
    sm_core.wait_send()
    for k in (1, 2, 3):
        sm_x(k).wait_send()
        sm_y(k).wait_send()
    bo_out.wait()
    so_out.wait()
    wo_out.wait()


def local(streams, stream_grads, branch_out, query_grads, query_weight, norm_gain, coef_weight, static_coef):
    any_spec = pl.BlockSpec(memory_space=pl.ANY)
    vmem = pl.BlockSpec(memory_space=pltpu.VMEM)
    smem = pl.BlockSpec(memory_space=pltpu.SMEM)
    dma = pltpu.SemaphoreType.DMA
    outs = pl.pallas_call(
        kernel,
        out_shape=(
            jax.ShapeDtypeStruct((4, T, F), BF16),
            jax.ShapeDtypeStruct((T, F), BF16),
            jax.ShapeDtypeStruct((RB, F), F32),
            jax.ShapeDtypeStruct((1, F), F32),
            jax.ShapeDtypeStruct((6, F), F32),
            jax.ShapeDtypeStruct((8, 128), F32),
        ),
        in_specs=[any_spec] * 5 + [vmem, vmem, smem],
        out_specs=(any_spec, any_spec, any_spec, vmem, vmem, vmem),
        scratch_shapes=[
            pltpu.VMEM((5, T, F), BF16),
            pltpu.VMEM((4, T, F), BF16),
            pltpu.VMEM((2, T, F), BF16),
            pltpu.VMEM((NZ, F, F), BF16),
            pltpu.VMEM((NZ, T, F), F32),
            pltpu.VMEM((2, 4, 2, T // 2, F), BF16),
            pltpu.VMEM((2, 4, 2, T // 2, F), BF16),
            pltpu.VMEM((NZ, 8, T), F32),
            pltpu.VMEM((NZ, 8, T), F32),
            pltpu.VMEM((NZ, 8, T), F32),
            pltpu.VMEM((NZ, 8, T), F32),
            pltpu.VMEM((T, F), F32),
            pltpu.VMEM((F, T), BF16),
            pltpu.VMEM((NZ, 2, 2, RB, T), BF16),
            pltpu.VMEM((T, 128), F32),
            pltpu.VMEM((T, 128), F32),
            pltpu.VMEM((4, 128, F), BF16),
            pltpu.VMEM((5, 2, 3, HB, F), BF16),
            pltpu.VMEM((5, 2, 3, HB, F), BF16),
            pltpu.VMEM((5, 2, HB, F), F32),
            pltpu.VMEM((NY, RB, F), F32),
            pltpu.VMEM((RB, F), F32),
            pltpu.VMEM((4, T, F), BF16),
            pltpu.VMEM((T, F), BF16),
            pltpu.VMEM((4, T, F), F32),
            pltpu.VMEM((16, F), F32),
            pltpu.VMEM((16, F), F32),
            pltpu.VMEM((NX, 16, F), F32),
            pltpu.VMEM((NY, 16, F), F32),
            dma((4,)),
            dma((NZ,)),
            dma((3,)),
            dma((2, 4, 2)),
            dma((2, 4, 2)),
            dma((2, 5, 2)),
            dma((2, 5, 2)),
            dma((3, NZ)),
            dma((3, NZ)),
            dma((3,)),
            dma((3,)),
            dma((5, 2, 3)),
            dma((5, 2, 3)),
            dma((7,)),
            dma((7,)),
        ],
        compiler_params=pltpu.CompilerParams(
            collective_id=0, has_side_effects=True, vmem_limit_bytes=56 * 1024 * 1024
        ),
        cost_estimate=pl.CostEstimate(flops=8_000_000_000, bytes_accessed=13_000_000, transcendentals=10000),
    )(
        streams,
        stream_grads,
        branch_out,
        query_grads,
        query_weight,
        norm_gain.reshape(1, F),
        coef_weight.T,
        static_coef,
    )
    so, bo, wo, gain, cwg, stat = outs
    return so, bo, wo, gain.reshape(F), cwg.T, stat[0:6, 0:4].T


def solution(mesh):
    in_specs = (
        P(None, "dp", "tensor"),
        P(None, "dp", "tensor"),
        P("dp", "tensor"),
        P("dp", "tensor"),
        P(None, "tensor"),
        P("tensor"),
        P("tensor", None),
        P(),
    )
    out_specs = (
        P(None, "dp", "tensor"),
        P("dp", "tensor"),
        P("dp", "tensor"),
        P("tensor"),
        P("tensor", None),
        P(),
    )
    return jax.shard_map(local, mesh=mesh, in_specs=in_specs, out_specs=out_specs, check_vma=False)
```

```python
import functools

import jax
import jax.numpy as jnp
from jax import lax
from jax.experimental import pallas as pl
from jax.experimental.pallas import tpu as pltpu
from jax.sharding import PartitionSpec as P

EPS = 1e-06
MESH = pl.DeviceIdType.MESH
F32 = jnp.float32
BF16 = jnp.bfloat16

T = 256
F = 640
NZ = 8
D = F * NZ
RB = 160
HB = RB // 2
NX = 4
NY = 4


def dot_nt(a, b):
    return lax.dot_general(a, b, (((1,), (1,)), ((), ())), preferred_element_type=F32)


def dot_nn(a, b):
    return lax.dot_general(a, b, (((1,), (0,)), ((), ())), preferred_element_type=F32)


def split3(v):
    hi = v.astype(BF16).astype(F32)
    rest = v - hi
    mid = rest.astype(BF16).astype(F32)
    return hi, mid, (rest - mid).astype(BF16).astype(F32)


def kernel(
    s_h, g_h, b_h, q_h, w_h, gain, cw, st,
    so_h, bo_h, wo_h, gain_o, cw_o, st_o,
    xs, gs, qq, wbuf,
    pbuf, rs_send, rs_recv,
    cl, r1, cfull, crit, crit_r, crit_f, hbuf,
    mixed, nts, nbuf, col1, colb, col2, cwx,
    xsend, xrecv, keep, xa, wo_v,
    so_v, bo_v, acc, sb, sc, sx, sy,
    in_sem, win_sem, out_sem,
    rs_ss, rs_rs, ag_ss, ag_rs, sync_ss, sync_rs, core_ss, core_rs, x_ss, x_rs, sm_ss, sm_rs,
):
    dp = lax.axis_index("dp")
    z = lax.axis_index("tensor")
    core = lax.rem(dp, 2)
    x = lax.rem(dp // 2, NX)
    y = dp // (2 * NX)

    def zdev(k):
        return (dp, lax.rem(z + k + NZ, NZ))

    def xdev(k):
        return ((y * NX + lax.rem(x + k + NX, NX)) * 2 + core, z)

    def ydev(k):
        return ((lax.rem(y + k + NY, NY) * NX + x) * 2 + core, z)

    cdev = (dp + 1 - 2 * core, z)

    def rcopy(src, dst, ss, rs, dev):
        return pltpu.make_async_remote_copy(
            src_ref=src, dst_ref=dst, send_sem=ss, recv_sem=rs, device_id=dev, device_id_type=MESH
        )

    gain_row = jnp.concatenate([gain[i : i + 1, :] for i in range(F // 128)], axis=1)

    q_in = pltpu.make_async_copy(q_h, qq.at[core], in_sem.at[0])
    s_in = pltpu.make_async_copy(s_h, xs.at[0:4], in_sem.at[1])
    g_in = pltpu.make_async_copy(g_h, gs, in_sem.at[2])
    b_in = pltpu.make_async_copy(b_h, xs.at[4], in_sem.at[3])

    def w_in(k):
        blk = lax.rem(z + k, NZ)
        return pltpu.make_async_copy(
            w_h.at[pl.ds(pl.multiple_of(blk * F, F), F)], wbuf.at[k], win_sem.at[k]
        )

    s_in.start()
    q_in.start()
    for k in (4, 3, 5):
        w_in(k).start()
    g_in.start()
    b_in.start()
    for k in (2, 6, 1, 7, 0):
        w_in(k).start()

    barrier = pltpu.get_barrier_semaphore()
    peers = [zdev(k) for k in range(1, NZ)] + [xdev(k) for k in (1, 2, 3)]
    peers += [ydev(k) for k in (1, 2, 3)] + [cdev]
    for dev in peers:
        pl.semaphore_signal(barrier, inc=1, device_id=dev, device_id_type=MESH)

    def rs_partial(k):
        w_in(k).wait()
        pbuf[k] = dot_nt(qq[core], wbuf[k])

    RIGHT, LEFT = 0, 1
    HALF = T // 2

    def rs_copy(way, step, half):
        return rcopy(
            rs_send.at[way, step, half],
            rs_recv.at[way, step, half],
            rs_ss.at[way, step, half],
            rs_rs.at[way, step, half],
            zdev(1 if way == RIGHT else -1),
        )

    def rs_block(way, step):
        return 4 - step if way == RIGHT else 4 + step if step else 4

    def rs_raw(way, step, half):
        rs_send[way, step, half] = pbuf[rs_block(way, step), half * HALF : (half + 1) * HALF].astype(BF16)
        rs_copy(way, step, half).start()

    def rs_add(way, step, half):
        rs_copy(way, step - 1, half).wait_recv()
        v = pbuf[rs_block(way, step), half * HALF : (half + 1) * HALF]
        rs_send[way, step, half] = (v + rs_recv[way, step - 1, half].astype(F32)).astype(BF16)
        rs_copy(way, step, half).start()

    s_in.wait()
    cw8 = jnp.concatenate([cw[...].astype(F32), jnp.zeros((10, F), F32)], axis=0).astype(BF16)
    rows_i = lax.broadcasted_iota(jnp.int32, (128, 128), 0)
    cols_i = lax.broadcasted_iota(jnp.int32, (128, 128), 1)
    eye = rows_i == cols_i

    def diag(block):
        return jnp.sum(jnp.where(eye, block, 0.0), axis=0, keepdims=True)

    def gram_s(blk, carry):
        at = pl.ds(pl.multiple_of(blk * 128, 128), 128)
        s_blk = xs[0:4, at, :].reshape(4 * 128, F)
        ss = dot_nt(s_blk, s_blk)
        gr = {
            (i, j): diag(ss[i * 128 : i * 128 + 128, j * 128 : j * 128 + 128])
            for i in range(4)
            for j in range(i, 4)
        }
        proj = dot_nt(cw8, s_blk)
        for i in range(4):
            cl[i, 0:7, at] = jnp.concatenate([proj[0:6, i * 128 : i * 128 + 128], gr[i, i]], axis=0)
        off = [gr[0, 1], gr[0, 2], gr[0, 3], gr[1, 2], gr[1, 3], gr[2, 3]]
        first = [proj[1:2, i * 128 : i * 128 + 128] for i in range(4)]
        first += [gr[i, i] for i in range(4)] + off + [jnp.zeros((1, 128), F32)] * 2
        for p in range(NZ):
            crit[p, :, at] = jnp.concatenate(first[2 * p : 2 * p + 2], axis=0)
        return carry

    def gram_g(blk, carry):
        at = pl.ds(pl.multiple_of(blk * 128, 128), 128)
        sb_blk = xs[:, at, :].reshape(5 * 128, F)
        g_blk = gs[:, at, :].reshape(4 * 128, F)
        sg = dot_nt(sb_blk, g_blk)
        route = [
            [diag(sg[i * 128 : i * 128 + 128, j * 128 : j * 128 + 128]) for j in range(4)] for i in range(5)
        ]
        for i in range(4):
            cl[i, 7:8, at] = route[4][i]
        for half in range(2):
            cl[4 + half, :, at] = jnp.concatenate(
                [route[2 * half + i][j] for i in range(2) for j in range(4)], axis=0
            )
        return carry

    lax.fori_loop(0, 2, gram_s, 0)
    for p in (6, 7):
        cl[p] = jnp.zeros((8, T), F32)

    def sync_out(k):
        return rcopy(
            cl.at[lax.rem(z + k, NZ)], r1.at[k], sync_ss.at[0, k], sync_rs.at[0, k], zdev(k)
        )

    def sync_back(k):
        return rcopy(cfull.at[z], cfull.at[z], sync_ss.at[1, k], sync_rs.at[1, k], zdev(k))

    def sync_back_in(k):
        at = cfull.at[lax.rem(z - k + NZ, NZ)]
        return rcopy(at, at, sync_ss.at[1, k], sync_rs.at[1, k], zdev(k))

    def crit_out(k):
        return rcopy(
            crit.at[lax.rem(z + k, NZ)], crit_r.at[k], sync_ss.at[3, k], sync_rs.at[3, k], zdev(k)
        )

    def crit_back(k):
        return rcopy(crit_f.at[z], crit_f.at[z], sync_ss.at[4, k], sync_rs.at[4, k], zdev(k))

    def crit_back_in(k):
        at = crit_f.at[lax.rem(z - k + NZ, NZ)]
        return rcopy(at, at, sync_ss.at[4, k], sync_rs.at[4, k], zdev(k))

    q_in.wait()
    for k in (4, 3, 5):
        rs_partial(k)

    pl.semaphore_wait(barrier, len(peers))
    for k in range(1, NZ):
        crit_out(k).start()
    rs_raw(RIGHT, 0, 0)
    rs_raw(LEFT, 0, 1)
    q_swap = rcopy(qq.at[core], qq.at[core], core_ss.at[0], core_rs.at[0], cdev)
    q_swap.start()
    rs_partial(2)
    first = crit[z]
    for k in range(1, NZ):
        crit_out(k).wait_recv()
        first = first + crit_r[k]
    crit_f[z] = first
    for k in range(1, NZ):
        crit_back(k).start()
    rs_raw(RIGHT, 1, 1)
    rs_raw(LEFT, 1, 0)
    g_in.wait()
    b_in.wait()
    lax.fori_loop(0, 2, gram_g, 0)

    cw_f = cw8[0:8].astype(F32)
    for i in range(4):
        parts = [cw_f, cw_f, cw_f]
        if i:
            parts = [jnp.zeros((i * 32, F), F32)] + parts
        parts = parts + [jnp.zeros((128 - i * 32 - 24, F), F32)]
        cwx[i] = jnp.concatenate(parts, axis=0).astype(BF16)

    row8 = lax.broadcasted_iota(jnp.int32, (8, T), 0)

    def coefficients():
        proj, inv, sq, cf = [], [], [], []
        at = {(0, 1): 8, (0, 2): 9, (0, 3): 10, (1, 2): 11, (1, 3): 12, (2, 3): 13}

        def g_of(i, j):
            r = 4 + i if i == j else at[min(i, j), max(i, j)]
            return crit_f[r // 2, r % 2 : r % 2 + 1]

        for i in range(4):
            piece = cfull[i]
            p8 = jnp.where(row8 < 6, piece, 0.0)
            iv = lax.rsqrt(g_of(i, i) / D + EPS)
            th = jnp.tanh(iv * p8)
            stc = jnp.zeros((8, T), F32)
            for c in range(6):
                stc = jnp.where(row8 == c, st[i, c], stc)
            proj.append(p8)
            inv.append(iv)
            sq.append(th)
            cf.append(stc + th)
        wid = [cf[i][1:2] for i in range(4)]
        gw = [sum(g_of(i, j) * wid[j] for j in range(4)) for i in range(4)]
        mixed_sq = sum(wid[i] * gw[i] for i in range(4))
        mix_inv = lax.rsqrt(mixed_sq / D + EPS)
        return proj, inv, sq, cf, wid, gw, mix_inv

    for k in range(1, NZ):
        crit_back_in(k).wait_recv()

    def mix_coefficients():
        low = jnp.concatenate([crit_f[p] for p in range(4)], axis=0)
        high = jnp.concatenate([crit_f[p] for p in range(4, 7)], axis=0)
        wid = [
            st[i, 1] + jnp.tanh(lax.rsqrt(low[4 + i : 5 + i] / D + EPS) * low[i : i + 1]) for i in range(4)
        ]
        at = {(0, 1): 0, (0, 2): 1, (0, 3): 2, (1, 2): 3, (1, 3): 4, (2, 3): 5}
        mixed_sq = sum(wid[i] * wid[i] * low[4 + i : 5 + i] for i in range(4))
        mixed_sq = mixed_sq + 2.0 * sum(wid[i] * wid[j] * high[r : r + 1] for (i, j), r in at.items())
        return wid, lax.rsqrt(mixed_sq / D + EPS)

    wid, mix_inv = mix_coefficients()
    col1[...] = jnp.concatenate(wid + [mix_inv, jnp.zeros((123, T), F32)], axis=0).T

    def mix(blk, carry):
        at = pl.ds(pl.multiple_of(blk * 32, 32), 32)
        c = col1[at, :]
        m = c[:, 0:1] * xs[0, at, :].astype(F32)
        for i in range(1, 4):
            m = m + c[:, i : i + 1] * xs[i, at, :].astype(F32)
        mixed[at, :] = m
        acc[0, at, :] = m * c[:, 4:5] * gain_row
        return carry

    lax.fori_loop(0, T // 32, mix, 0)
    for lane in range(F // 128):
        tr = acc[0, :, lane * 128 : lane * 128 + 128].T.astype(BF16)
        nts[lane * 128 : lane * 128 + 128, :] = tr

    def n_swap(kk):
        return rcopy(
            nts.at[pl.ds(pl.multiple_of((2 * kk + 1 - core) * RB, 32), RB)],
            nbuf.at[z, kk, core],
            core_ss.at[1 + kk],
            core_rs.at[1 + kk],
            cdev,
        )

    def n_swap_in(kk):
        return rcopy(
            nts.at[pl.ds(pl.multiple_of((2 * kk + 1 - core) * RB, 32), RB)],
            nbuf.at[z, kk, 1 - core],
            core_ss.at[1 + kk],
            core_rs.at[1 + kk],
            cdev,
        )

    for kk in range(2):
        n_swap(kk).start()
    for kk in range(2):
        nbuf[z, kk, core] = nts[pl.ds(pl.multiple_of((2 * kk + core) * RB, 32), RB), :]

    rs_add(RIGHT, 1, 0)
    rs_add(LEFT, 1, 1)

    def ag_copy(way, step, kk):
        blk = lax.rem(z - step + 1 + NZ, NZ) if way == RIGHT else lax.rem(z + step - 1, NZ)
        at = nbuf.at[blk, kk]
        return rcopy(at, at, ag_ss.at[way, step, kk], ag_rs.at[way, step, kk], zdev(1 if way == RIGHT else -1))

    def ag_in(way, step, kk):
        blk = lax.rem(z - step + NZ, NZ) if way == RIGHT else lax.rem(z + step, NZ)
        at = nbuf.at[blk, kk]
        return rcopy(at, at, ag_ss.at[way, step, kk], ag_rs.at[way, step, kk], zdev(1 if way == RIGHT else -1))

    n_swap_in(0).wait_recv()
    ag_copy(RIGHT, 1, 0).start()
    n_swap_in(1).wait_recv()
    ag_copy(LEFT, 1, 1).start()
    ag_copy(RIGHT, 1, 1).start()
    ag_copy(LEFT, 1, 0).start()

    def ag_forward(step):
        for first in range(2):
            for way in (RIGHT, LEFT):
                kk = first ^ way
                if step < 4 or kk == way:
                    ag_in(way, step - 1, kk).wait_recv()
                    ag_copy(way, step, kk).start()

    par = lax.rem(z, 2)
    z0 = z - par
    q_swap_in = rcopy(qq.at[1 - core], qq.at[1 - core], core_ss.at[0], core_rs.at[0], cdev)

    def pair_base(m):
        if m == 0:
            return z0
        if m == 3:
            return lax.rem(z0 + 4, NZ)
        sign = -1 if m == 1 else 1
        return lax.rem(z0 + sign * 2 * (1 - 2 * par) + NZ, NZ)

    def wg_block(m, r):
        xd = lax.rem(x + r, NX)
        n = nbuf.at[lax.rem(pair_base(m) + xd // 2, NZ), lax.rem(xd, 2)]
        return dot_nn(n[0], qq[0]) + dot_nn(n[1], qq[1])

    def red_copy(e, way, part):
        dev = (xdev if e < 4 else ydev)(1 if way == RIGHT else -1)
        return rcopy(
            xsend.at[e, way, part], xrecv.at[e, way, part], x_ss.at[e, way, part], x_rs.at[e, way, part], dev
        )

    def red_start(e, block):
        far = block(2).astype(BF16)
        xsend[e, RIGHT, 0] = far[:HB]
        red_copy(e, RIGHT, 0).start()
        xsend[e, LEFT, 0] = far[HB:]
        red_copy(e, LEFT, 0).start()
        near = block(1)
        xsend[e, RIGHT, 1] = near[HB:].astype(BF16)
        red_copy(e, RIGHT, 1).start()
        keep[e, RIGHT] = near[:HB]
        near = block(3)
        xsend[e, LEFT, 1] = near[:HB].astype(BF16)
        red_copy(e, LEFT, 1).start()
        keep[e, LEFT] = near[HB:]

    def red_forward(e):
        for way in (RIGHT, LEFT):
            red_copy(e, way, 0).wait_recv()
            xsend[e, way, 2] = (keep[e, way] + xrecv[e, way, 0].astype(F32)).astype(BF16)
            red_copy(e, way, 2).start()

    def red_finish(e, own):
        for way in (RIGHT, LEFT):
            for part in (1, 2):
                red_copy(e, way, part).wait_recv()
        top = own[:HB] + xrecv[e, RIGHT, 2].astype(F32) + xrecv[e, LEFT, 1].astype(F32)
        low = own[HB:] + xrecv[e, RIGHT, 1].astype(F32) + xrecv[e, LEFT, 2].astype(F32)
        return top, low

    def pair_start(m):
        red_start(m, functools.partial(wg_block, m))
        xa[pair_base(m) // 2] = wg_block(m, 0)

    def pair_finish(m):
        at = pair_base(m) // 2
        top, low = red_finish(m, xa[at])
        xa[at, :HB] = top
        xa[at, HB:] = low

    def branch(blk, carry):
        at = pl.ds(pl.multiple_of(blk * 32, 32), 32)
        c = colb[at, :]
        v = c[:, 0:1] * gs[0, at, :].astype(F32)
        for j in range(1, 4):
            v = v + c[:, j : j + 1] * gs[j, at, :].astype(F32)
        bo_v[at, :] = v.astype(BF16)
        return carry

    rs_partial(6)
    rs_add(RIGHT, 2, 1)
    rs_add(LEFT, 2, 0)
    for k in (1, 7, 0):
        rs_partial(k)
    q_swap_in.wait_recv()

    ag_forward(2)
    rs_add(RIGHT, 2, 0)
    rs_add(LEFT, 2, 1)
    pair_start(0)

    red_forward(0)

    ag_forward(3)
    pair_start(1)
    red_forward(1)

    ag_forward(4)
    for half in (1, 0):
        for way in (RIGHT, LEFT):
            rs_add(way, 3, half)
    for k in range(1, NZ):
        sync_out(k).start()
    ag_in(RIGHT, 3, 1).wait_recv()
    ag_in(LEFT, 3, 0).wait_recv()
    pair_start(2)
    pair_finish(0)
    red_forward(2)

    ag_in(RIGHT, 4, 0).wait_recv()
    ag_in(LEFT, 4, 1).wait_recv()
    pair_start(3)
    pair_finish(1)
    pair_finish(2)

    def norm(blk):
        at = slice(blk * 128, blk * 128 + 128)
        for way in (RIGHT, LEFT):
            rs_copy(way, 3, blk).wait_recv()
        ng = pbuf[0, at, :] + rs_recv[RIGHT, 3, blk].astype(F32) + rs_recv[LEFT, 3, blk].astype(F32)
        gain_sum = jnp.sum(ng * (mixed[at, :] * col1[at, 4:5]), axis=0, keepdims=True)
        scaled = ng * gain_row
        pbuf[0, at, :] = scaled
        hi, mid, lo = split3(scaled)
        parts = jnp.concatenate([hi, mid, lo], axis=0).astype(BF16)
        prod = dot_nt(xs[0:4, at, :].reshape(4 * 128, F), parts)
        h = []
        for i in range(4):
            p = prod[i * 128 : i * 128 + 128]
            h.append(diag(p[:, 0:128] + p[:, 128:256] + p[:, 256:384]))
        hbuf[z, 4 * blk : 4 * blk + 4, :] = jnp.concatenate(h, axis=0)
        return gain_sum

    gain_part = norm(1)
    total = cl[z]
    for k in range(1, NZ):
        sync_out(k).wait_recv()
        total = total + r1[k]
    cfull[z] = total
    gain_part = gain_part + norm(0)

    def h_out(k):
        return rcopy(hbuf.at[z], hbuf.at[z], sync_ss.at[2, k], sync_rs.at[2, k], zdev(k))

    def h_in(k):
        at = hbuf.at[lax.rem(z - k + NZ, NZ)]
        return rcopy(at, at, sync_ss.at[2, k], sync_rs.at[2, k], zdev(k))

    for k in range(1, NZ):
        h_out(k).start()
    for k in range(1, NZ):
        sync_back(k).start()

    red_forward(3)
    pair_finish(3)
    red_start(4, lambda r: xa[lax.rem(y + r, NY)])

    for k in range(1, NZ):
        h_in(k).wait_recv()
    for k in range(1, NZ):
        sync_back_in(k).wait_recv()

    proj, inv, sq, cf, wid, gw, mix_inv = coefficients()
    h8 = hbuf[0]
    for k in range(1, NZ):
        h8 = h8 + hbuf[k]
    h8 = jnp.concatenate([h8[0:4], h8[4:8]], axis=1)
    inner = sum(wid[i] * h8[i : i + 1] for i in range(4))
    kfac = mix_inv * mix_inv * mix_inv * inner / D
    rows, left = [], []
    sub8 = lax.broadcasted_iota(jnp.int32, (8, 128), 0)
    lane8 = lax.broadcasted_iota(jnp.int32, (8, 128), 1)
    stat = jnp.zeros((1, 128), F32)
    for i in range(4):
        mix_grad = mix_inv * h8[i : i + 1] - kfac * gw[i]
        route = cfull[4 + i // 2][4 * (i % 2) : 4 * (i % 2) + 4]
        cg = jnp.concatenate([cfull[i][7:8], mix_grad, route, jnp.zeros((2, T), F32)], axis=0)
        pre = cg * (1.0 - sq[i] * sq[i])
        pg = pre * inv[i]
        scale = jnp.sum(pre * proj[i], axis=0, keepdims=True) * (inv[i] * inv[i] * inv[i] / D)
        hi, mid, lo = split3(pg)
        left.append(jnp.concatenate([hi, mid, lo], axis=0))
        rows += [hi, mid, lo, wid[i], scale, cf[i][2:6], mix_inv, kfac]
        sums = jnp.broadcast_to(jnp.sum(cg, axis=1, keepdims=True), (8, 128))
        stat = stat + jnp.sum(jnp.where(lane8 == sub8 + 8 * i, sums, 0.0), axis=0, keepdims=True)
    col2[...] = jnp.concatenate(rows, axis=0).T
    cpart = dot_nn(jnp.concatenate(left, axis=1).astype(BF16), xs[0:4].reshape(4 * T, F))
    cpart = cpart[0:8] + cpart[8:16] + cpart[16:24]
    last = jnp.concatenate([stat, jnp.zeros((1, F - 128), F32)], axis=1)
    sb[...] = jnp.concatenate([cpart[0:6], gain_part, last], axis=0)

    sm_core = rcopy(sb, sc, sm_ss.at[0], sm_rs.at[0], cdev)
    sm_core.start()

    lhs = col2[...].astype(BF16)
    for i in range(4):
        acc[i] = dot_nn(lhs, cwx[i])

    def out_rows(blk, carry):
        at = pl.ds(pl.multiple_of(blk * 16, 16), 16)
        c = col2[at, :]
        mg = c[:, 30:31] * pbuf[0, at, :] - c[:, 31:32] * mixed[at, :]
        g = [gs[j, at, :].astype(F32) for j in range(4)]
        for i in range(4):
            o = 32 * i + 24
            v = acc[i, at, :] + c[:, o : o + 1] * mg - c[:, o + 1 : o + 2] * xs[i, at, :].astype(F32)
            for j in range(4):
                v = v + c[:, o + 2 + j : o + 3 + j] * g[j]
            so_v[i, at, :] = v.astype(BF16)
        return carry

    def sm_x(k):
        return rcopy(sx.at[x], sx.at[x], sm_ss.at[k], sm_rs.at[k], xdev(k))

    def sm_x_in(k):
        at = sx.at[lax.rem(x - k + NX, NX)]
        return rcopy(at, at, sm_ss.at[k], sm_rs.at[k], xdev(k))

    def sm_y(k):
        return rcopy(sy.at[y], sy.at[y], sm_ss.at[3 + k], sm_rs.at[3 + k], ydev(k))

    def sm_y_in(k):
        at = sy.at[lax.rem(y - k + NY, NY)]
        return rcopy(at, at, sm_ss.at[3 + k], sm_rs.at[3 + k], ydev(k))

    sm_core.wait_recv()
    sx[x] = sb[...] + sc[...]
    for k in (1, 2, 3):
        sm_x(k).start()
    red_forward(4)

    lax.fori_loop(0, T // 32, out_rows, 0)
    for k in (1, 2, 3):
        sm_x_in(k).wait_recv()
    sy[y] = sx[0] + sx[1] + sx[2] + sx[3]
    for k in (1, 2, 3):
        sm_y(k).start()
    lax.fori_loop(T // 32, T // 16, out_rows, 0)
    colb[...] = jnp.concatenate([cf[j][0:1] for j in range(4)] + [jnp.zeros((124, T), F32)], axis=0).T
    lax.fori_loop(0, T // 32, branch, 0)
    bo_out = pltpu.make_async_copy(bo_v, bo_h, out_sem.at[0])
    bo_out.start()
    so_out = pltpu.make_async_copy(so_v, so_h, out_sem.at[1])
    so_out.start()

    top, low = red_finish(4, xa[y])
    wo_v[:HB] = top
    wo_v[HB:] = low
    wo_out = pltpu.make_async_copy(wo_v, wo_h, out_sem.at[2])
    wo_out.start()

    for k in (1, 2, 3):
        sm_y_in(k).wait_recv()
    small = sy[0] + sy[1] + sy[2] + sy[3]
    cw_o[...] = small[0:6]
    gain_o[...] = jnp.concatenate([small[6:7, i * 128 : i * 128 + 128] for i in range(F // 128)], axis=0)
    st_o[...] = jnp.concatenate([small[7:8, 8 * i : 8 * i + 6] for i in range(4)], axis=0)

    for way in (RIGHT, LEFT):
        for step in range(4):
            for half in range(2):
                if step or half == way:
                    rs_copy(way, step, half).wait_send()
        for step in range(1, 5):
            for kk in range(2):
                if step < 4 or kk == way:
                    ag_copy(way, step, kk).wait_send()
        for e in range(5):
            for part in range(3):
                red_copy(e, way, part).wait_send()
    for k in range(1, NZ):
        sync_out(k).wait_send()
        sync_back(k).wait_send()
        crit_out(k).wait_send()
        crit_back(k).wait_send()
        h_out(k).wait_send()
    q_swap.wait_send()
    for kk in range(2):
        n_swap(kk).wait_send()
    sm_core.wait_send()
    for k in (1, 2, 3):
        sm_x(k).wait_send()
        sm_y(k).wait_send()
    bo_out.wait()
    so_out.wait()
    wo_out.wait()


def copy_kernel(*refs):
    src, dst, held, sem = refs[:6], refs[6:12], refs[12:15], refs[15]
    pieces = [(0, (i, pl.ds(h, T // 2))) for i in range(4) for h in (0, T // 2)]
    pieces += [(1, (pl.ds(h, T // 2),)) for h in (0, T // 2)]
    pieces += [(2, (pl.ds(h, HB),)) for h in (0, HB)]
    loads = [
        pltpu.make_async_copy(src[i].at[at], held[i].at[at], sem.at[0, n]) for n, (i, at) in enumerate(pieces)
    ]
    stores = [
        pltpu.make_async_copy(held[i].at[at], dst[i].at[at], sem.at[1, n]) for n, (i, at) in enumerate(pieces)
    ]
    for c in loads:
        c.start()
    for i in range(3, 6):
        dst[i][...] = src[i][...]
    for load, store in zip(loads, stores):
        load.wait()
        store.start()
    for c in stores:
        c.wait()


def local(streams, stream_grads, branch_out, query_grads, query_weight, norm_gain, coef_weight, static_coef):
    any_spec = pl.BlockSpec(memory_space=pl.ANY)
    vmem = pl.BlockSpec(memory_space=pltpu.VMEM)
    smem = pl.BlockSpec(memory_space=pltpu.SMEM)
    dma = pltpu.SemaphoreType.DMA
    outs = pl.pallas_call(
        kernel,
        out_shape=(
            jax.ShapeDtypeStruct((4, T, F), BF16),
            jax.ShapeDtypeStruct((T, F), BF16),
            jax.ShapeDtypeStruct((RB, F), F32),
            jax.ShapeDtypeStruct((F // 128, 128), F32),
            jax.ShapeDtypeStruct((6, F), F32),
            jax.ShapeDtypeStruct((4, 6), F32),
        ),
        in_specs=[any_spec] * 5 + [vmem, vmem, smem],
        out_specs=(any_spec, any_spec, any_spec, vmem, vmem, vmem),
        scratch_shapes=[
            pltpu.VMEM((5, T, F), BF16),
            pltpu.VMEM((4, T, F), BF16),
            pltpu.VMEM((2, T, F), BF16),
            pltpu.VMEM((NZ, F, F), BF16),
            pltpu.VMEM((NZ, T, F), F32),
            pltpu.VMEM((2, 4, 2, T // 2, F), BF16),
            pltpu.VMEM((2, 4, 2, T // 2, F), BF16),
            pltpu.VMEM((NZ, 8, T), F32),
            pltpu.VMEM((NZ, 8, T), F32),
            pltpu.VMEM((NZ, 8, T), F32),
            pltpu.VMEM((NZ, 2, T), F32),
            pltpu.VMEM((NZ, 2, T), F32),
            pltpu.VMEM((NZ, 2, T), F32),
            pltpu.VMEM((NZ, 8, 128), F32),
            pltpu.VMEM((T, F), F32),
            pltpu.VMEM((F, T), BF16),
            pltpu.VMEM((NZ, 2, 2, RB, T), BF16),
            pltpu.VMEM((T, 128), F32),
            pltpu.VMEM((T, 128), F32),
            pltpu.VMEM((T, 128), F32),
            pltpu.VMEM((4, 128, F), BF16),
            pltpu.VMEM((5, 2, 3, HB, F), BF16),
            pltpu.VMEM((5, 2, 3, HB, F), BF16),
            pltpu.VMEM((5, 2, HB, F), F32),
            pltpu.VMEM((NY, RB, F), F32),
            pltpu.VMEM((RB, F), F32),
            pltpu.VMEM((4, T, F), BF16),
            pltpu.VMEM((T, F), BF16),
            pltpu.VMEM((4, T, F), F32),
            pltpu.VMEM((8, F), F32),
            pltpu.VMEM((8, F), F32),
            pltpu.VMEM((NX, 8, F), F32),
            pltpu.VMEM((NY, 8, F), F32),
            dma((4,)),
            dma((NZ,)),
            dma((3,)),
            dma((2, 4, 2)),
            dma((2, 4, 2)),
            dma((2, 5, 2)),
            dma((2, 5, 2)),
            dma((5, NZ)),
            dma((5, NZ)),
            dma((3,)),
            dma((3,)),
            dma((5, 2, 3)),
            dma((5, 2, 3)),
            dma((7,)),
            dma((7,)),
        ],
        compiler_params=pltpu.CompilerParams(
            collective_id=0, has_side_effects=True, vmem_limit_bytes=56 * 1024 * 1024
        ),
        cost_estimate=pl.CostEstimate(flops=8_000_000_000, bytes_accessed=13_000_000, transcendentals=10000),
    )(
        streams,
        stream_grads,
        branch_out,
        query_grads,
        query_weight,
        norm_gain.reshape(F // 128, 128),
        coef_weight.T,
        static_coef,
    )
    so, bo, wo, gain, cwg, stat = pl.pallas_call(
        copy_kernel,
        out_shape=[jax.ShapeDtypeStruct(o.shape, o.dtype) for o in outs],
        in_specs=[any_spec] * 3 + [vmem] * 3,
        out_specs=[any_spec] * 3 + [vmem] * 3,
        scratch_shapes=[pltpu.VMEM(o.shape, o.dtype) for o in outs[:3]] + [dma((2, 12))],
        compiler_params=pltpu.CompilerParams(vmem_limit_bytes=60 * 1024 * 1024),
    )(*outs)
    return so, bo, wo, gain.reshape(F), cwg.T, stat


def solution(mesh):
    in_specs = (
        P(None, "dp", "tensor"),
        P(None, "dp", "tensor"),
        P("dp", "tensor"),
        P("dp", "tensor"),
        P(None, "tensor"),
        P("tensor"),
        P("tensor", None),
        P(),
    )
    out_specs = (
        P(None, "dp", "tensor"),
        P("dp", "tensor"),
        P("dp", "tensor"),
        P("tensor"),
        P("tensor", None),
        P(),
    )
    return jax.shard_map(local, mesh=mesh, in_specs=in_specs, out_specs=out_specs, check_vma=False)
```

```python
import functools

import jax
import jax.numpy as jnp
from jax import lax
from jax.experimental import pallas as pl
from jax.experimental.pallas import tpu as pltpu
from jax.sharding import PartitionSpec as P

EPS = 1e-06
MESH = pl.DeviceIdType.MESH
F32 = jnp.float32
BF16 = jnp.bfloat16

T = 256
F = 640
NZ = 8
D = F * NZ
RB = 160
HB = RB // 2
NX = 4
NY = 4


def dot_nt(a, b):
    return lax.dot_general(a, b, (((1,), (1,)), ((), ())), preferred_element_type=F32)


def dot_nn(a, b):
    return lax.dot_general(a, b, (((1,), (0,)), ((), ())), preferred_element_type=F32)


def split3(v):
    hi = v.astype(BF16).astype(F32)
    rest = v - hi
    mid = rest.astype(BF16).astype(F32)
    return hi, mid, (rest - mid).astype(BF16).astype(F32)


def kernel(
    s_h, g_h, b_h, q_h, w_h, gain, cw, st,
    so_v, bo_v, wo_v, gain_o, cw_o, st_o,
    xs, gs, qq, wbuf,
    pbuf, rs_send, rs_recv,
    cl, r1, cfull, crit, crit_r, crit_f, hbuf,
    mixed, nts, nbuf, col1, colb, col2, cwx,
    xsend, xrecv, keep, xa,
    acc, sb, sc, sx, sy,
    in_sem, win_sem,
    rs_ss, rs_rs, ag_ss, ag_rs, sync_ss, sync_rs, core_ss, core_rs, x_ss, x_rs, sm_ss, sm_rs,
):
    dp = lax.axis_index("dp")
    z = lax.axis_index("tensor")
    core = lax.rem(dp, 2)
    x = lax.rem(dp // 2, NX)
    y = dp // (2 * NX)

    def zdev(k):
        return (dp, lax.rem(z + k + NZ, NZ))

    def xdev(k):
        return ((y * NX + lax.rem(x + k + NX, NX)) * 2 + core, z)

    def ydev(k):
        return ((lax.rem(y + k + NY, NY) * NX + x) * 2 + core, z)

    cdev = (dp + 1 - 2 * core, z)

    def rcopy(src, dst, ss, rs, dev):
        return pltpu.make_async_remote_copy(
            src_ref=src, dst_ref=dst, send_sem=ss, recv_sem=rs, device_id=dev, device_id_type=MESH
        )

    gain_row = jnp.concatenate([gain[i : i + 1, :] for i in range(F // 128)], axis=1)

    q_in = pltpu.make_async_copy(q_h, qq.at[core], in_sem.at[0])
    s_in = pltpu.make_async_copy(s_h, xs.at[0:4], in_sem.at[1])
    g_in = pltpu.make_async_copy(g_h, gs, in_sem.at[2])
    b_in = pltpu.make_async_copy(b_h, xs.at[4], in_sem.at[3])

    def w_in(k):
        blk = lax.rem(z + k, NZ)
        return pltpu.make_async_copy(
            w_h.at[pl.ds(pl.multiple_of(blk * F, F), F)], wbuf.at[k], win_sem.at[k]
        )

    s_in.start()
    q_in.start()
    for k in (4, 3, 5):
        w_in(k).start()
    g_in.start()
    b_in.start()
    for k in (2, 6, 1, 7, 0):
        w_in(k).start()

    barrier = pltpu.get_barrier_semaphore()
    peers = [zdev(k) for k in range(1, NZ)] + [xdev(k) for k in (1, 2, 3)]
    peers += [ydev(k) for k in (1, 2, 3)] + [cdev]
    for dev in peers:
        pl.semaphore_signal(barrier, inc=1, device_id=dev, device_id_type=MESH)

    def rs_partial(k):
        w_in(k).wait()
        pbuf[k] = dot_nt(qq[core], wbuf[k])

    RIGHT, LEFT = 0, 1
    HALF = T // 2

    def rs_copy(way, step, half):
        return rcopy(
            rs_send.at[way, step, half],
            rs_recv.at[way, step, half],
            rs_ss.at[way, step, half],
            rs_rs.at[way, step, half],
            zdev(1 if way == RIGHT else -1),
        )

    def rs_block(way, step):
        return 4 - step if way == RIGHT else 4 + step if step else 4

    def rs_raw(way, step, half):
        rs_send[way, step, half] = pbuf[rs_block(way, step), half * HALF : (half + 1) * HALF].astype(BF16)
        rs_copy(way, step, half).start()

    def rs_add(way, step, half):
        rs_copy(way, step - 1, half).wait_recv()
        v = pbuf[rs_block(way, step), half * HALF : (half + 1) * HALF]
        rs_send[way, step, half] = (v + rs_recv[way, step - 1, half].astype(F32)).astype(BF16)
        rs_copy(way, step, half).start()

    s_in.wait()
    cw8 = jnp.concatenate([cw[...].astype(F32), jnp.zeros((10, F), F32)], axis=0).astype(BF16)
    rows_i = lax.broadcasted_iota(jnp.int32, (128, 128), 0)
    cols_i = lax.broadcasted_iota(jnp.int32, (128, 128), 1)
    eye = rows_i == cols_i

    def diag(block):
        return jnp.sum(jnp.where(eye, block, 0.0), axis=0, keepdims=True)

    def gram_s(blk, carry):
        at = pl.ds(pl.multiple_of(blk * 128, 128), 128)
        s_blk = xs[0:4, at, :].reshape(4 * 128, F)
        ss = dot_nt(s_blk, s_blk)
        gr = {
            (i, j): diag(ss[i * 128 : i * 128 + 128, j * 128 : j * 128 + 128])
            for i in range(4)
            for j in range(i, 4)
        }
        proj = dot_nt(cw8, s_blk)
        for i in range(4):
            cl[i, 0:7, at] = jnp.concatenate([proj[0:6, i * 128 : i * 128 + 128], gr[i, i]], axis=0)
        off = [gr[0, 1], gr[0, 2], gr[0, 3], gr[1, 2], gr[1, 3], gr[2, 3]]
        first = [proj[1:2, i * 128 : i * 128 + 128] for i in range(4)]
        first += [gr[i, i] for i in range(4)] + off + [jnp.zeros((1, 128), F32)] * 2
        for p in range(NZ):
            crit[p, :, at] = jnp.concatenate(first[2 * p : 2 * p + 2], axis=0)
        return carry

    def gram_g(blk, carry):
        at = pl.ds(pl.multiple_of(blk * 128, 128), 128)
        sb_blk = xs[:, at, :].reshape(5 * 128, F)
        g_blk = gs[:, at, :].reshape(4 * 128, F)
        sg = dot_nt(sb_blk, g_blk)
        route = [
            [diag(sg[i * 128 : i * 128 + 128, j * 128 : j * 128 + 128]) for j in range(4)] for i in range(5)
        ]
        for i in range(4):
            cl[i, 7:8, at] = route[4][i]
        for half in range(2):
            cl[4 + half, :, at] = jnp.concatenate(
                [route[2 * half + i][j] for i in range(2) for j in range(4)], axis=0
            )
        return carry

    lax.fori_loop(0, 2, gram_s, 0)
    for p in (6, 7):
        cl[p] = jnp.zeros((8, T), F32)

    def sync_out(k):
        return rcopy(
            cl.at[lax.rem(z + k, NZ)], r1.at[k], sync_ss.at[0, k], sync_rs.at[0, k], zdev(k)
        )

    def sync_back(k):
        return rcopy(cfull.at[z], cfull.at[z], sync_ss.at[1, k], sync_rs.at[1, k], zdev(k))

    def sync_back_in(k):
        at = cfull.at[lax.rem(z - k + NZ, NZ)]
        return rcopy(at, at, sync_ss.at[1, k], sync_rs.at[1, k], zdev(k))

    def crit_out(k):
        return rcopy(
            crit.at[lax.rem(z + k, NZ)], crit_r.at[k], sync_ss.at[3, k], sync_rs.at[3, k], zdev(k)
        )

    def crit_back(k):
        return rcopy(crit_f.at[z], crit_f.at[z], sync_ss.at[4, k], sync_rs.at[4, k], zdev(k))

    def crit_back_in(k):
        at = crit_f.at[lax.rem(z - k + NZ, NZ)]
        return rcopy(at, at, sync_ss.at[4, k], sync_rs.at[4, k], zdev(k))

    q_in.wait()
    for k in (4, 3, 5):
        rs_partial(k)

    pl.semaphore_wait(barrier, len(peers))
    for k in range(1, NZ):
        crit_out(k).start()
    rs_raw(RIGHT, 0, 0)
    rs_raw(LEFT, 0, 1)
    q_swap = rcopy(qq.at[core], qq.at[core], core_ss.at[0], core_rs.at[0], cdev)
    q_swap.start()
    rs_partial(2)
    first = crit[z]
    for k in range(1, NZ):
        crit_out(k).wait_recv()
        first = first + crit_r[k]
    crit_f[z] = first
    for k in range(1, NZ):
        crit_back(k).start()
    rs_raw(RIGHT, 1, 1)
    rs_raw(LEFT, 1, 0)
    g_in.wait()
    b_in.wait()
    lax.fori_loop(0, 2, gram_g, 0)

    cw_f = cw8[0:8].astype(F32)
    for i in range(4):
        parts = [cw_f, cw_f, cw_f]
        if i:
            parts = [jnp.zeros((i * 32, F), F32)] + parts
        parts = parts + [jnp.zeros((128 - i * 32 - 24, F), F32)]
        cwx[i] = jnp.concatenate(parts, axis=0).astype(BF16)

    row8 = lax.broadcasted_iota(jnp.int32, (8, T), 0)

    def coefficients():
        proj, inv, sq, cf = [], [], [], []
        at = {(0, 1): 8, (0, 2): 9, (0, 3): 10, (1, 2): 11, (1, 3): 12, (2, 3): 13}

        def g_of(i, j):
            r = 4 + i if i == j else at[min(i, j), max(i, j)]
            return crit_f[r // 2, r % 2 : r % 2 + 1]

        for i in range(4):
            piece = cfull[i]
            p8 = jnp.where(row8 < 6, piece, 0.0)
            iv = lax.rsqrt(g_of(i, i) / D + EPS)
            th = jnp.tanh(iv * p8)
            stc = jnp.zeros((8, T), F32)
            for c in range(6):
                stc = jnp.where(row8 == c, st[i, c], stc)
            proj.append(p8)
            inv.append(iv)
            sq.append(th)
            cf.append(stc + th)
        wid = [cf[i][1:2] for i in range(4)]
        gw = [sum(g_of(i, j) * wid[j] for j in range(4)) for i in range(4)]
        mixed_sq = sum(wid[i] * gw[i] for i in range(4))
        mix_inv = lax.rsqrt(mixed_sq / D + EPS)
        return proj, inv, sq, cf, wid, gw, mix_inv

    rs_add(RIGHT, 1, 0)
    rs_add(LEFT, 1, 1)
    for k in range(1, NZ):
        crit_back_in(k).wait_recv()

    def mix_coefficients():
        low = jnp.concatenate([crit_f[p] for p in range(4)], axis=0)
        high = jnp.concatenate([crit_f[p] for p in range(4, 7)], axis=0)
        wid = [
            st[i, 1] + jnp.tanh(lax.rsqrt(low[4 + i : 5 + i] / D + EPS) * low[i : i + 1]) for i in range(4)
        ]
        at = {(0, 1): 0, (0, 2): 1, (0, 3): 2, (1, 2): 3, (1, 3): 4, (2, 3): 5}
        mixed_sq = sum(wid[i] * wid[i] * low[4 + i : 5 + i] for i in range(4))
        mixed_sq = mixed_sq + 2.0 * sum(wid[i] * wid[j] * high[r : r + 1] for (i, j), r in at.items())
        return wid, lax.rsqrt(mixed_sq / D + EPS)

    wid, mix_inv = mix_coefficients()
    col1[...] = jnp.concatenate(wid + [mix_inv, jnp.zeros((123, T), F32)], axis=0).T

    def mix(blk, carry):
        at = pl.ds(pl.multiple_of(blk * 32, 32), 32)
        c = col1[at, :]
        m = c[:, 0:1] * xs[0, at, :].astype(F32)
        for i in range(1, 4):
            m = m + c[:, i : i + 1] * xs[i, at, :].astype(F32)
        mixed[at, :] = m
        acc[0, at, :] = m * c[:, 4:5] * gain_row
        return carry

    lax.fori_loop(0, T // 32, mix, 0)
    for lane in range(F // 128):
        tr = acc[0, :, lane * 128 : lane * 128 + 128].T.astype(BF16)
        nts[lane * 128 : lane * 128 + 128, :] = tr

    def n_swap(kk):
        return rcopy(
            nts.at[pl.ds(pl.multiple_of((2 * kk + 1 - core) * RB, 32), RB)],
            nbuf.at[z, kk, core],
            core_ss.at[1 + kk],
            core_rs.at[1 + kk],
            cdev,
        )

    def n_swap_in(kk):
        return rcopy(
            nts.at[pl.ds(pl.multiple_of((2 * kk + 1 - core) * RB, 32), RB)],
            nbuf.at[z, kk, 1 - core],
            core_ss.at[1 + kk],
            core_rs.at[1 + kk],
            cdev,
        )

    for kk in range(2):
        n_swap(kk).start()
    for kk in range(2):
        nbuf[z, kk, core] = nts[pl.ds(pl.multiple_of((2 * kk + core) * RB, 32), RB), :]

    def ag_copy(way, step, kk):
        blk = lax.rem(z - step + 1 + NZ, NZ) if way == RIGHT else lax.rem(z + step - 1, NZ)
        at = nbuf.at[blk, kk]
        return rcopy(at, at, ag_ss.at[way, step, kk], ag_rs.at[way, step, kk], zdev(1 if way == RIGHT else -1))

    def ag_in(way, step, kk):
        blk = lax.rem(z - step + NZ, NZ) if way == RIGHT else lax.rem(z + step, NZ)
        at = nbuf.at[blk, kk]
        return rcopy(at, at, ag_ss.at[way, step, kk], ag_rs.at[way, step, kk], zdev(1 if way == RIGHT else -1))

    n_swap_in(0).wait_recv()
    ag_copy(RIGHT, 1, 0).start()
    n_swap_in(1).wait_recv()
    ag_copy(LEFT, 1, 1).start()
    ag_copy(RIGHT, 1, 1).start()
    ag_copy(LEFT, 1, 0).start()

    def ag_forward(step):
        for first in range(2):
            for way in (RIGHT, LEFT):
                kk = first ^ way
                if step < 4 or kk == way:
                    ag_in(way, step - 1, kk).wait_recv()
                    ag_copy(way, step, kk).start()

    par = lax.rem(z, 2)
    z0 = z - par
    q_swap_in = rcopy(qq.at[1 - core], qq.at[1 - core], core_ss.at[0], core_rs.at[0], cdev)

    def pair_base(m):
        if m == 0:
            return z0
        if m == 3:
            return lax.rem(z0 + 4, NZ)
        sign = -1 if m == 1 else 1
        return lax.rem(z0 + sign * 2 * (1 - 2 * par) + NZ, NZ)

    def wg_block(m, r):
        xd = lax.rem(x + r, NX)
        n = nbuf.at[lax.rem(pair_base(m) + xd // 2, NZ), lax.rem(xd, 2)]
        return dot_nn(n[0], qq[0]) + dot_nn(n[1], qq[1])

    def red_copy(e, way, part):
        dev = (xdev if e < 4 else ydev)(1 if way == RIGHT else -1)
        return rcopy(
            xsend.at[e, way, part], xrecv.at[e, way, part], x_ss.at[e, way, part], x_rs.at[e, way, part], dev
        )

    def red_start(e, block):
        far = block(2).astype(BF16)
        xsend[e, RIGHT, 0] = far[:HB]
        red_copy(e, RIGHT, 0).start()
        xsend[e, LEFT, 0] = far[HB:]
        red_copy(e, LEFT, 0).start()
        near = block(1)
        xsend[e, RIGHT, 1] = near[HB:].astype(BF16)
        red_copy(e, RIGHT, 1).start()
        keep[e, RIGHT] = near[:HB]
        near = block(3)
        xsend[e, LEFT, 1] = near[:HB].astype(BF16)
        red_copy(e, LEFT, 1).start()
        keep[e, LEFT] = near[HB:]

    def red_forward(e):
        for way in (RIGHT, LEFT):
            red_copy(e, way, 0).wait_recv()
            xsend[e, way, 2] = (keep[e, way] + xrecv[e, way, 0].astype(F32)).astype(BF16)
            red_copy(e, way, 2).start()

    def red_finish(e, own):
        for way in (RIGHT, LEFT):
            for part in (1, 2):
                red_copy(e, way, part).wait_recv()
        top = own[:HB] + xrecv[e, RIGHT, 2].astype(F32) + xrecv[e, LEFT, 1].astype(F32)
        low = own[HB:] + xrecv[e, RIGHT, 1].astype(F32) + xrecv[e, LEFT, 2].astype(F32)
        return top, low

    def pair_start(m):
        red_start(m, functools.partial(wg_block, m))
        xa[pair_base(m) // 2] = wg_block(m, 0)

    def pair_finish(m):
        at = pair_base(m) // 2
        top, low = red_finish(m, xa[at])
        xa[at, :HB] = top
        xa[at, HB:] = low

    def branch(blk, carry):
        at = pl.ds(pl.multiple_of(blk * 32, 32), 32)
        c = colb[at, :]
        v = c[:, 0:1] * gs[0, at, :].astype(F32)
        for j in range(1, 4):
            v = v + c[:, j : j + 1] * gs[j, at, :].astype(F32)
        bo_v[at, :] = v.astype(BF16)
        return carry

    rs_partial(6)
    rs_add(RIGHT, 2, 1)
    rs_add(LEFT, 2, 0)
    for k in (1, 7, 0):
        rs_partial(k)
    q_swap_in.wait_recv()

    ag_forward(2)
    rs_add(RIGHT, 2, 0)
    rs_add(LEFT, 2, 1)
    pair_start(0)

    red_forward(0)

    ag_forward(3)
    pair_start(1)
    red_forward(1)

    ag_forward(4)
    for half in (1, 0):
        for way in (RIGHT, LEFT):
            rs_add(way, 3, half)
    for k in range(1, NZ):
        sync_out(k).start()
    ag_in(RIGHT, 3, 1).wait_recv()
    ag_in(LEFT, 3, 0).wait_recv()
    pair_start(2)
    pair_finish(0)
    red_forward(2)

    ag_in(RIGHT, 4, 0).wait_recv()
    ag_in(LEFT, 4, 1).wait_recv()
    pair_start(3)
    pair_finish(1)
    pair_finish(2)

    def norm(blk):
        at = slice(blk * 128, blk * 128 + 128)
        for way in (RIGHT, LEFT):
            rs_copy(way, 3, blk).wait_recv()
        ng = pbuf[0, at, :] + rs_recv[RIGHT, 3, blk].astype(F32) + rs_recv[LEFT, 3, blk].astype(F32)
        gain_sum = jnp.sum(ng * (mixed[at, :] * col1[at, 4:5]), axis=0, keepdims=True)
        scaled = ng * gain_row
        pbuf[0, at, :] = scaled
        hi, mid, lo = split3(scaled)
        parts = jnp.concatenate([hi, mid, lo], axis=0).astype(BF16)
        prod = dot_nt(xs[0:4, at, :].reshape(4 * 128, F), parts)
        h = []
        for i in range(4):
            p = prod[i * 128 : i * 128 + 128]
            h.append(diag(p[:, 0:128] + p[:, 128:256] + p[:, 256:384]))
        hbuf[z, 4 * blk : 4 * blk + 4, :] = jnp.concatenate(h, axis=0)
        return gain_sum

    gain_part = norm(1)
    gain_part = gain_part + norm(0)

    def h_out(k):
        return rcopy(hbuf.at[z], hbuf.at[z], sync_ss.at[2, k], sync_rs.at[2, k], zdev(k))

    def h_in(k):
        at = hbuf.at[lax.rem(z - k + NZ, NZ)]
        return rcopy(at, at, sync_ss.at[2, k], sync_rs.at[2, k], zdev(k))

    for k in range(1, NZ):
        h_out(k).start()
    total = cl[z]
    for k in range(1, NZ):
        sync_out(k).wait_recv()
        total = total + r1[k]
    cfull[z] = total
    for k in range(1, NZ):
        sync_back(k).start()

    red_forward(3)
    pair_finish(3)
    red_start(4, lambda r: xa[lax.rem(y + r, NY)])

    for k in range(1, NZ):
        h_in(k).wait_recv()
    for k in range(1, NZ):
        sync_back_in(k).wait_recv()

    proj, inv, sq, cf, wid, gw, mix_inv = coefficients()
    h8 = hbuf[0]
    for k in range(1, NZ):
        h8 = h8 + hbuf[k]
    h8 = jnp.concatenate([h8[0:4], h8[4:8]], axis=1)
    inner = sum(wid[i] * h8[i : i + 1] for i in range(4))
    kfac = mix_inv * mix_inv * mix_inv * inner / D
    rows, left = [], []
    sub8 = lax.broadcasted_iota(jnp.int32, (8, 128), 0)
    lane8 = lax.broadcasted_iota(jnp.int32, (8, 128), 1)
    stat = jnp.zeros((1, 128), F32)
    for i in range(4):
        mix_grad = mix_inv * h8[i : i + 1] - kfac * gw[i]
        route = cfull[4 + i // 2][4 * (i % 2) : 4 * (i % 2) + 4]
        cg = jnp.concatenate([cfull[i][7:8], mix_grad, route, jnp.zeros((2, T), F32)], axis=0)
        pre = cg * (1.0 - sq[i] * sq[i])
        pg = pre * inv[i]
        scale = jnp.sum(pre * proj[i], axis=0, keepdims=True) * (inv[i] * inv[i] * inv[i] / D)
        hi, mid, lo = split3(pg)
        left.append(jnp.concatenate([hi, mid, lo], axis=0))
        rows += [hi, mid, lo, wid[i], scale, cf[i][2:6], mix_inv, kfac]
        sums = jnp.broadcast_to(jnp.sum(cg, axis=1, keepdims=True), (8, 128))
        stat = stat + jnp.sum(jnp.where(lane8 == sub8 + 8 * i, sums, 0.0), axis=0, keepdims=True)
    col2[...] = jnp.concatenate(rows, axis=0).T
    cpart = dot_nn(jnp.concatenate(left, axis=1).astype(BF16), xs[0:4].reshape(4 * T, F))
    cpart = cpart[0:8] + cpart[8:16] + cpart[16:24]
    last = jnp.concatenate([stat, jnp.zeros((1, F - 128), F32)], axis=1)
    sb[...] = jnp.concatenate([cpart[0:6], gain_part, last], axis=0)

    sm_core = rcopy(sb, sc, sm_ss.at[0], sm_rs.at[0], cdev)
    sm_core.start()

    lhs = col2[...].astype(BF16)
    for i in range(4):
        acc[i] = dot_nn(lhs, cwx[i])

    def out_rows(blk, carry):
        at = pl.ds(pl.multiple_of(blk * 16, 16), 16)
        c = col2[at, :]
        mg = c[:, 30:31] * pbuf[0, at, :] - c[:, 31:32] * mixed[at, :]
        g = [gs[j, at, :].astype(F32) for j in range(4)]
        for i in range(4):
            o = 32 * i + 24
            v = acc[i, at, :] + c[:, o : o + 1] * mg - c[:, o + 1 : o + 2] * xs[i, at, :].astype(F32)
            for j in range(4):
                v = v + c[:, o + 2 + j : o + 3 + j] * g[j]
            so_v[i, at, :] = v.astype(BF16)
        return carry

    def sm_x(k):
        return rcopy(sx.at[x], sx.at[x], sm_ss.at[k], sm_rs.at[k], xdev(k))

    def sm_x_in(k):
        at = sx.at[lax.rem(x - k + NX, NX)]
        return rcopy(at, at, sm_ss.at[k], sm_rs.at[k], xdev(k))

    def sm_y(k):
        return rcopy(sy.at[y], sy.at[y], sm_ss.at[3 + k], sm_rs.at[3 + k], ydev(k))

    def sm_y_in(k):
        at = sy.at[lax.rem(y - k + NY, NY)]
        return rcopy(at, at, sm_ss.at[3 + k], sm_rs.at[3 + k], ydev(k))

    sm_core.wait_recv()
    sx[x] = sb[...] + sc[...]
    for k in (1, 2, 3):
        sm_x(k).start()
    red_forward(4)

    lax.fori_loop(0, T // 32, out_rows, 0)
    for k in (1, 2, 3):
        sm_x_in(k).wait_recv()
    sy[y] = sx[0] + sx[1] + sx[2] + sx[3]
    for k in (1, 2, 3):
        sm_y(k).start()
    lax.fori_loop(T // 32, T // 16, out_rows, 0)
    colb[...] = jnp.concatenate([cf[j][0:1] for j in range(4)] + [jnp.zeros((124, T), F32)], axis=0).T
    lax.fori_loop(0, T // 32, branch, 0)

    top, low = red_finish(4, xa[y])
    wo_v[:HB] = top
    wo_v[HB:] = low

    for k in (1, 2, 3):
        sm_y_in(k).wait_recv()
    small = sy[0] + sy[1] + sy[2] + sy[3]
    cw_o[...] = small[0:6]
    gain_o[...] = jnp.concatenate([small[6:7, i * 128 : i * 128 + 128] for i in range(F // 128)], axis=0)
    st_o[...] = jnp.concatenate([small[7:8, 8 * i : 8 * i + 6] for i in range(4)], axis=0)

    for way in (RIGHT, LEFT):
        for step in range(4):
            for half in range(2):
                if step or half == way:
                    rs_copy(way, step, half).wait_send()
        for step in range(1, 5):
            for kk in range(2):
                if step < 4 or kk == way:
                    ag_copy(way, step, kk).wait_send()
        for e in range(5):
            for part in range(3):
                red_copy(e, way, part).wait_send()
    for k in range(1, NZ):
        sync_out(k).wait_send()
        sync_back(k).wait_send()
        crit_out(k).wait_send()
        crit_back(k).wait_send()
        h_out(k).wait_send()
    q_swap.wait_send()
    for kk in range(2):
        n_swap(kk).wait_send()
    sm_core.wait_send()
    for k in (1, 2, 3):
        sm_x(k).wait_send()
        sm_y(k).wait_send()


def copy_kernel(*refs):
    src, dst, sem = refs[:6], refs[6:12], refs[12]
    copies = [pltpu.make_async_copy(src[i], dst[i], sem.at[i]) for i in range(6)]
    for c in copies:
        c.start()
    for c in copies:
        c.wait()


def local(streams, stream_grads, branch_out, query_grads, query_weight, norm_gain, coef_weight, static_coef):
    any_spec = pl.BlockSpec(memory_space=pl.ANY)
    vmem = pl.BlockSpec(memory_space=pltpu.VMEM)
    smem = pl.BlockSpec(memory_space=pltpu.SMEM)
    dma = pltpu.SemaphoreType.DMA
    outs = pl.pallas_call(
        kernel,
        out_shape=(
            pltpu.VMEM((4, T, F), BF16),
            pltpu.VMEM((T, F), BF16),
            pltpu.VMEM((RB, F), F32),
            pltpu.VMEM((F // 128, 128), F32),
            pltpu.VMEM((6, F), F32),
            pltpu.VMEM((4, 6), F32),
        ),
        in_specs=[any_spec] * 5 + [vmem, vmem, smem],
        out_specs=(vmem,) * 6,
        scratch_shapes=[
            pltpu.VMEM((5, T, F), BF16),
            pltpu.VMEM((4, T, F), BF16),
            pltpu.VMEM((2, T, F), BF16),
            pltpu.VMEM((NZ, F, F), BF16),
            pltpu.VMEM((NZ, T, F), F32),
            pltpu.VMEM((2, 4, 2, T // 2, F), BF16),
            pltpu.VMEM((2, 4, 2, T // 2, F), BF16),
            pltpu.VMEM((NZ, 8, T), F32),
            pltpu.VMEM((NZ, 8, T), F32),
            pltpu.VMEM((NZ, 8, T), F32),
            pltpu.VMEM((NZ, 2, T), F32),
            pltpu.VMEM((NZ, 2, T), F32),
            pltpu.VMEM((NZ, 2, T), F32),
            pltpu.VMEM((NZ, 8, 128), F32),
            pltpu.VMEM((T, F), F32),
            pltpu.VMEM((F, T), BF16),
            pltpu.VMEM((NZ, 2, 2, RB, T), BF16),
            pltpu.VMEM((T, 128), F32),
            pltpu.VMEM((T, 128), F32),
            pltpu.VMEM((T, 128), F32),
            pltpu.VMEM((4, 128, F), BF16),
            pltpu.VMEM((5, 2, 3, HB, F), BF16),
            pltpu.VMEM((5, 2, 3, HB, F), BF16),
            pltpu.VMEM((5, 2, HB, F), F32),
            pltpu.VMEM((NY, RB, F), F32),
            pltpu.VMEM((4, T, F), F32),
            pltpu.VMEM((8, F), F32),
            pltpu.VMEM((8, F), F32),
            pltpu.VMEM((NX, 8, F), F32),
            pltpu.VMEM((NY, 8, F), F32),
            dma((4,)),
            dma((NZ,)),
            dma((2, 4, 2)),
            dma((2, 4, 2)),
            dma((2, 5, 2)),
            dma((2, 5, 2)),
            dma((5, NZ)),
            dma((5, NZ)),
            dma((3,)),
            dma((3,)),
            dma((5, 2, 3)),
            dma((5, 2, 3)),
            dma((7,)),
            dma((7,)),
        ],
        compiler_params=pltpu.CompilerParams(
            collective_id=0, has_side_effects=True, vmem_limit_bytes=56 * 1024 * 1024
        ),
        cost_estimate=pl.CostEstimate(flops=8_000_000_000, bytes_accessed=13_000_000, transcendentals=10000),
    )(
        streams,
        stream_grads,
        branch_out,
        query_grads,
        query_weight,
        norm_gain.reshape(F // 128, 128),
        coef_weight.T,
        static_coef,
    )
    so, bo, wo, gain, cwg, stat = pl.pallas_call(
        copy_kernel,
        out_shape=[jax.ShapeDtypeStruct(o.shape, o.dtype) for o in outs],
        in_specs=[any_spec] * 6,
        out_specs=[any_spec] * 6,
        scratch_shapes=[dma((6,))],
        compiler_params=pltpu.CompilerParams(vmem_limit_bytes=1024 * 1024),
    )(*outs)
    return so, bo, wo, gain.reshape(F), cwg.T, stat


def solution(mesh):
    in_specs = (
        P(None, "dp", "tensor"),
        P(None, "dp", "tensor"),
        P("dp", "tensor"),
        P("dp", "tensor"),
        P(None, "tensor"),
        P("tensor"),
        P("tensor", None),
        P(),
    )
    out_specs = (
        P(None, "dp", "tensor"),
        P("dp", "tensor"),
        P("dp", "tensor"),
        P("tensor"),
        P("tensor", None),
        P(),
    )
    return jax.shard_map(local, mesh=mesh, in_specs=in_specs, out_specs=out_specs, check_vma=False)
```

```python
import functools

import jax
import jax.numpy as jnp
from jax import lax
from jax.experimental import pallas as pl
from jax.experimental.pallas import tpu as pltpu
from jax.sharding import PartitionSpec as P

EPS = 1e-06
MESH = pl.DeviceIdType.MESH
F32 = jnp.float32
BF16 = jnp.bfloat16

T = 256
F = 640
NZ = 8
D = F * NZ
RB = 160
HB = RB // 2
NX = 4
NY = 4


def dot_nt(a, b):
    return lax.dot_general(a, b, (((1,), (1,)), ((), ())), preferred_element_type=F32)


def dot_nn(a, b):
    return lax.dot_general(a, b, (((1,), (0,)), ((), ())), preferred_element_type=F32)


def split3(v):
    hi = v.astype(BF16).astype(F32)
    rest = v - hi
    mid = rest.astype(BF16).astype(F32)
    return hi, mid, (rest - mid).astype(BF16).astype(F32)


def kernel(
    s_h, g_h, b_h, q_h, w_h, gain, cw, st,
    so_v, bo_v, wo_v, gain_o, cw_o, st_o,
    xs, gs, qq, wbuf,
    pbuf, rs_send, rs_recv,
    cl, r1, cfull, crit, crit_r, crit_f, hbuf,
    mixed, nts, nbuf, col1, colb, col2, cwx,
    xsend, xrecv, keep, xa,
    acc, sb, sc, sx, sy,
    in_sem, win_sem,
    rs_ss, rs_rs, ag_ss, ag_rs, sync_ss, sync_rs, core_ss, core_rs, x_ss, x_rs, sm_ss, sm_rs,
):
    dp = lax.axis_index("dp")
    z = lax.axis_index("tensor")
    core = lax.rem(dp, 2)
    x = lax.rem(dp // 2, NX)
    y = dp // (2 * NX)

    def zdev(k):
        return (dp, lax.rem(z + k + NZ, NZ))

    def xdev(k):
        return ((y * NX + lax.rem(x + k + NX, NX)) * 2 + core, z)

    def ydev(k):
        return ((lax.rem(y + k + NY, NY) * NX + x) * 2 + core, z)

    cdev = (dp + 1 - 2 * core, z)

    def rcopy(src, dst, ss, rs, dev):
        return pltpu.make_async_remote_copy(
            src_ref=src, dst_ref=dst, send_sem=ss, recv_sem=rs, device_id=dev, device_id_type=MESH
        )

    gain_row = jnp.concatenate([gain[i : i + 1, :] for i in range(F // 128)], axis=1)

    q_in = pltpu.make_async_copy(q_h, qq.at[core], in_sem.at[0])
    s_in = pltpu.make_async_copy(s_h, xs.at[0:4], in_sem.at[1])
    g_in = pltpu.make_async_copy(g_h, gs, in_sem.at[2])
    b_in = pltpu.make_async_copy(b_h, xs.at[4], in_sem.at[3])

    def w_in(k):
        blk = lax.rem(z + k, NZ)
        return pltpu.make_async_copy(
            w_h.at[pl.ds(pl.multiple_of(blk * F, F), F)], wbuf.at[k], win_sem.at[k]
        )

    s_in.start()
    q_in.start()
    for k in (4, 3, 5):
        w_in(k).start()
    g_in.start()
    b_in.start()
    for k in (2, 6, 1, 7, 0):
        w_in(k).start()

    barrier = pltpu.get_barrier_semaphore()
    peers = [zdev(k) for k in range(1, NZ)] + [xdev(k) for k in (1, 2, 3)]
    peers += [ydev(k) for k in (1, 2, 3)] + [cdev]
    for dev in peers:
        pl.semaphore_signal(barrier, inc=1, device_id=dev, device_id_type=MESH)

    def rs_partial(k):
        w_in(k).wait()
        pbuf[k] = dot_nt(qq[core], wbuf[k])

    RIGHT, LEFT = 0, 1
    HALF = T // 2

    def rs_copy(way, step, half):
        return rcopy(
            rs_send.at[way, step, half],
            rs_recv.at[way, step, half],
            rs_ss.at[way, step, half],
            rs_rs.at[way, step, half],
            zdev(1 if way == RIGHT else -1),
        )

    def rs_block(way, step):
        return 4 - step if way == RIGHT else 4 + step if step else 4

    def rs_raw(way, step, half):
        rs_send[way, step, half] = pbuf[rs_block(way, step), half * HALF : (half + 1) * HALF].astype(BF16)
        rs_copy(way, step, half).start()

    def rs_add(way, step, half):
        rs_copy(way, step - 1, half).wait_recv()
        v = pbuf[rs_block(way, step), half * HALF : (half + 1) * HALF]
        rs_send[way, step, half] = (v + rs_recv[way, step - 1, half].astype(F32)).astype(BF16)
        rs_copy(way, step, half).start()

    s_in.wait()
    cw8 = jnp.concatenate([cw[...].astype(F32), jnp.zeros((10, F), F32)], axis=0).astype(BF16)
    rows_i = lax.broadcasted_iota(jnp.int32, (128, 128), 0)
    cols_i = lax.broadcasted_iota(jnp.int32, (128, 128), 1)
    eye = rows_i == cols_i

    def diag(block):
        return jnp.sum(jnp.where(eye, block, 0.0), axis=0, keepdims=True)

    def gram_s(blk, carry):
        at = pl.ds(pl.multiple_of(blk * 128, 128), 128)
        s_blk = xs[0:4, at, :].reshape(4 * 128, F)
        ss = dot_nt(s_blk, s_blk)
        gr = {
            (i, j): diag(ss[i * 128 : i * 128 + 128, j * 128 : j * 128 + 128])
            for i in range(4)
            for j in range(i, 4)
        }
        proj = dot_nt(cw8, s_blk)
        for i in range(4):
            cl[i, 0:7, at] = jnp.concatenate([proj[0:6, i * 128 : i * 128 + 128], gr[i, i]], axis=0)
        off = [gr[0, 1], gr[0, 2], gr[0, 3], gr[1, 2], gr[1, 3], gr[2, 3]]
        first = [proj[1:2, i * 128 : i * 128 + 128] for i in range(4)]
        first += [gr[i, i] for i in range(4)] + off + [jnp.zeros((1, 128), F32)] * 2
        for p in range(NZ):
            crit[p, :, at] = jnp.concatenate(first[2 * p : 2 * p + 2], axis=0)
        return carry

    def gram_g(blk, carry):
        at = pl.ds(pl.multiple_of(blk * 128, 128), 128)
        sb_blk = xs[:, at, :].reshape(5 * 128, F)
        g_blk = gs[:, at, :].reshape(4 * 128, F)
        sg = dot_nt(sb_blk, g_blk)
        route = [
            [diag(sg[i * 128 : i * 128 + 128, j * 128 : j * 128 + 128]) for j in range(4)] for i in range(5)
        ]
        for i in range(4):
            cl[i, 7:8, at] = route[4][i]
        for half in range(2):
            cl[4 + half, :, at] = jnp.concatenate(
                [route[2 * half + i][j] for i in range(2) for j in range(4)], axis=0
            )
        return carry

    lax.fori_loop(0, 2, gram_s, 0)
    for p in (6, 7):
        cl[p] = jnp.zeros((8, T), F32)

    def sync_out(k):
        return rcopy(
            cl.at[lax.rem(z + k, NZ)], r1.at[k], sync_ss.at[0, k], sync_rs.at[0, k], zdev(k)
        )

    def sync_back(k):
        return rcopy(cfull.at[z], cfull.at[z], sync_ss.at[1, k], sync_rs.at[1, k], zdev(k))

    def sync_back_in(k):
        at = cfull.at[lax.rem(z - k + NZ, NZ)]
        return rcopy(at, at, sync_ss.at[1, k], sync_rs.at[1, k], zdev(k))

    def crit_out(k):
        return rcopy(
            crit.at[lax.rem(z + k, NZ)], crit_r.at[k], sync_ss.at[3, k], sync_rs.at[3, k], zdev(k)
        )

    def crit_back(k):
        return rcopy(crit_f.at[z], crit_f.at[z], sync_ss.at[4, k], sync_rs.at[4, k], zdev(k))

    def crit_back_in(k):
        at = crit_f.at[lax.rem(z - k + NZ, NZ)]
        return rcopy(at, at, sync_ss.at[4, k], sync_rs.at[4, k], zdev(k))

    q_in.wait()
    rs_partial(4)

    pl.semaphore_wait(barrier, len(peers))
    for k in range(1, NZ):
        crit_out(k).start()
    rs_raw(RIGHT, 0, 0)
    rs_raw(LEFT, 0, 1)
    q_swap = rcopy(qq.at[core], qq.at[core], core_ss.at[0], core_rs.at[0], cdev)
    q_swap.start()
    rs_partial(3)
    rs_partial(5)
    first = crit[z]
    for k in range(1, NZ):
        crit_out(k).wait_recv()
        first = first + crit_r[k]
    crit_f[z] = first
    for k in range(1, NZ):
        crit_back(k).start()
    rs_raw(RIGHT, 1, 1)
    rs_raw(LEFT, 1, 0)
    rs_partial(2)
    rs_partial(6)
    g_in.wait()
    b_in.wait()
    lax.fori_loop(0, 2, gram_g, 0)

    cw_f = cw8[0:8].astype(F32)
    for i in range(4):
        parts = [cw_f, cw_f, cw_f]
        if i:
            parts = [jnp.zeros((i * 32, F), F32)] + parts
        parts = parts + [jnp.zeros((128 - i * 32 - 24, F), F32)]
        cwx[i] = jnp.concatenate(parts, axis=0).astype(BF16)

    row8 = lax.broadcasted_iota(jnp.int32, (8, T), 0)

    def coefficients():
        proj, inv, sq, cf = [], [], [], []
        at = {(0, 1): 8, (0, 2): 9, (0, 3): 10, (1, 2): 11, (1, 3): 12, (2, 3): 13}

        def g_of(i, j):
            r = 4 + i if i == j else at[min(i, j), max(i, j)]
            return crit_f[r // 2, r % 2 : r % 2 + 1]

        for i in range(4):
            piece = cfull[i]
            p8 = jnp.where(row8 < 6, piece, 0.0)
            iv = lax.rsqrt(g_of(i, i) / D + EPS)
            th = jnp.tanh(iv * p8)
            stc = jnp.zeros((8, T), F32)
            for c in range(6):
                stc = jnp.where(row8 == c, st[i, c], stc)
            proj.append(p8)
            inv.append(iv)
            sq.append(th)
            cf.append(stc + th)
        wid = [cf[i][1:2] for i in range(4)]
        gw = [sum(g_of(i, j) * wid[j] for j in range(4)) for i in range(4)]
        mixed_sq = sum(wid[i] * gw[i] for i in range(4))
        mix_inv = lax.rsqrt(mixed_sq / D + EPS)
        return proj, inv, sq, cf, wid, gw, mix_inv

    rs_add(RIGHT, 1, 0)
    rs_add(LEFT, 1, 1)
    for k in range(1, NZ):
        crit_back_in(k).wait_recv()

    def mix_coefficients():
        low = jnp.concatenate([crit_f[p] for p in range(4)], axis=0)
        high = jnp.concatenate([crit_f[p] for p in range(4, 7)], axis=0)
        wid = [
            st[i, 1] + jnp.tanh(lax.rsqrt(low[4 + i : 5 + i] / D + EPS) * low[i : i + 1]) for i in range(4)
        ]
        at = {(0, 1): 0, (0, 2): 1, (0, 3): 2, (1, 2): 3, (1, 3): 4, (2, 3): 5}
        mixed_sq = sum(wid[i] * wid[i] * low[4 + i : 5 + i] for i in range(4))
        mixed_sq = mixed_sq + 2.0 * sum(wid[i] * wid[j] * high[r : r + 1] for (i, j), r in at.items())
        return wid, lax.rsqrt(mixed_sq / D + EPS)

    wid, mix_inv = mix_coefficients()
    col1[...] = jnp.concatenate(wid + [mix_inv, jnp.zeros((123, T), F32)], axis=0).T

    def mix(blk, carry):
        at = pl.ds(pl.multiple_of(blk * 32, 32), 32)
        c = col1[at, :]
        m = c[:, 0:1] * xs[0, at, :].astype(F32)
        for i in range(1, 4):
            m = m + c[:, i : i + 1] * xs[i, at, :].astype(F32)
        mixed[at, :] = m
        acc[0, at, :] = m * c[:, 4:5] * gain_row
        return carry

    lax.fori_loop(0, T // 32, mix, 0)
    for lane in range(F // 128):
        tr = acc[0, :, lane * 128 : lane * 128 + 128].T.astype(BF16)
        nts[lane * 128 : lane * 128 + 128, :] = tr

    def n_swap(kk):
        return rcopy(
            nts.at[pl.ds(pl.multiple_of((2 * kk + 1 - core) * RB, 32), RB)],
            nbuf.at[z, kk, core],
            core_ss.at[1 + kk],
            core_rs.at[1 + kk],
            cdev,
        )

    def n_swap_in(kk):
        return rcopy(
            nts.at[pl.ds(pl.multiple_of((2 * kk + 1 - core) * RB, 32), RB)],
            nbuf.at[z, kk, 1 - core],
            core_ss.at[1 + kk],
            core_rs.at[1 + kk],
            cdev,
        )

    for kk in range(2):
        n_swap(kk).start()
    for kk in range(2):
        nbuf[z, kk, core] = nts[pl.ds(pl.multiple_of((2 * kk + core) * RB, 32), RB), :]

    def ag_copy(way, step, kk):
        blk = lax.rem(z - step + 1 + NZ, NZ) if way == RIGHT else lax.rem(z + step - 1, NZ)
        at = nbuf.at[blk, kk]
        return rcopy(at, at, ag_ss.at[way, step, kk], ag_rs.at[way, step, kk], zdev(1 if way == RIGHT else -1))

    def ag_in(way, step, kk):
        blk = lax.rem(z - step + NZ, NZ) if way == RIGHT else lax.rem(z + step, NZ)
        at = nbuf.at[blk, kk]
        return rcopy(at, at, ag_ss.at[way, step, kk], ag_rs.at[way, step, kk], zdev(1 if way == RIGHT else -1))

    n_swap_in(0).wait_recv()
    ag_copy(RIGHT, 1, 0).start()
    n_swap_in(1).wait_recv()
    ag_copy(LEFT, 1, 1).start()
    ag_copy(RIGHT, 1, 1).start()
    ag_copy(LEFT, 1, 0).start()

    def ag_forward(step):
        for first in range(2):
            for way in (RIGHT, LEFT):
                kk = first ^ way
                if step < 4 or kk == way:
                    ag_in(way, step - 1, kk).wait_recv()
                    ag_copy(way, step, kk).start()

    par = lax.rem(z, 2)
    z0 = z - par
    q_swap_in = rcopy(qq.at[1 - core], qq.at[1 - core], core_ss.at[0], core_rs.at[0], cdev)

    def pair_base(m):
        if m == 0:
            return z0
        if m == 3:
            return lax.rem(z0 + 4, NZ)
        sign = -1 if m == 1 else 1
        return lax.rem(z0 + sign * 2 * (1 - 2 * par) + NZ, NZ)

    def wg_block(m, r):
        xd = lax.rem(x + r, NX)
        n = nbuf.at[lax.rem(pair_base(m) + xd // 2, NZ), lax.rem(xd, 2)]
        return dot_nn(n[0], qq[0]) + dot_nn(n[1], qq[1])

    def red_copy(e, way, part):
        dev = (xdev if e < 4 else ydev)(1 if way == RIGHT else -1)
        return rcopy(
            xsend.at[e, way, part], xrecv.at[e, way, part], x_ss.at[e, way, part], x_rs.at[e, way, part], dev
        )

    def red_start(e, block):
        far = block(2).astype(BF16)
        xsend[e, RIGHT, 0] = far[:HB]
        red_copy(e, RIGHT, 0).start()
        xsend[e, LEFT, 0] = far[HB:]
        red_copy(e, LEFT, 0).start()
        near = block(1)
        xsend[e, RIGHT, 1] = near[HB:].astype(BF16)
        red_copy(e, RIGHT, 1).start()
        keep[e, RIGHT] = near[:HB]
        near = block(3)
        xsend[e, LEFT, 1] = near[:HB].astype(BF16)
        red_copy(e, LEFT, 1).start()
        keep[e, LEFT] = near[HB:]

    def red_forward(e):
        for way in (RIGHT, LEFT):
            red_copy(e, way, 0).wait_recv()
            xsend[e, way, 2] = (keep[e, way] + xrecv[e, way, 0].astype(F32)).astype(BF16)
            red_copy(e, way, 2).start()

    def red_finish(e, own):
        for way in (RIGHT, LEFT):
            for part in (1, 2):
                red_copy(e, way, part).wait_recv()
        top = own[:HB] + xrecv[e, RIGHT, 2].astype(F32) + xrecv[e, LEFT, 1].astype(F32)
        low = own[HB:] + xrecv[e, RIGHT, 1].astype(F32) + xrecv[e, LEFT, 2].astype(F32)
        return top, low

    def pair_start(m):
        red_start(m, functools.partial(wg_block, m))
        xa[pair_base(m) // 2] = wg_block(m, 0)

    def pair_finish(m):
        at = pair_base(m) // 2
        top, low = red_finish(m, xa[at])
        xa[at, :HB] = top
        xa[at, HB:] = low

    def branch(blk, carry):
        at = pl.ds(pl.multiple_of(blk * 32, 32), 32)
        c = colb[at, :]
        v = c[:, 0:1] * gs[0, at, :].astype(F32)
        for j in range(1, 4):
            v = v + c[:, j : j + 1] * gs[j, at, :].astype(F32)
        bo_v[at, :] = v.astype(BF16)
        return carry

    rs_add(RIGHT, 2, 1)
    rs_add(LEFT, 2, 0)
    for k in (1, 7, 0):
        rs_partial(k)
    q_swap_in.wait_recv()

    ag_forward(2)
    rs_add(RIGHT, 2, 0)
    rs_add(LEFT, 2, 1)
    pair_start(0)

    red_forward(0)

    ag_forward(3)
    pair_start(1)
    red_forward(1)

    ag_forward(4)
    for half in (1, 0):
        for way in (RIGHT, LEFT):
            rs_add(way, 3, half)
    for k in range(1, NZ):
        sync_out(k).start()
    ag_in(RIGHT, 3, 1).wait_recv()
    ag_in(LEFT, 3, 0).wait_recv()
    pair_start(2)
    pair_finish(0)
    red_forward(2)

    ag_in(RIGHT, 4, 0).wait_recv()
    ag_in(LEFT, 4, 1).wait_recv()
    pair_start(3)
    pair_finish(1)

    def norm(blk):
        at = slice(blk * 128, blk * 128 + 128)
        for way in (RIGHT, LEFT):
            rs_copy(way, 3, blk).wait_recv()
        ng = pbuf[0, at, :] + rs_recv[RIGHT, 3, blk].astype(F32) + rs_recv[LEFT, 3, blk].astype(F32)
        gain_sum = jnp.sum(ng * (mixed[at, :] * col1[at, 4:5]), axis=0, keepdims=True)
        scaled = ng * gain_row
        pbuf[0, at, :] = scaled
        hi, mid, lo = split3(scaled)
        parts = jnp.concatenate([hi, mid, lo], axis=0).astype(BF16)
        prod = dot_nt(xs[0:4, at, :].reshape(4 * 128, F), parts)
        h = []
        for i in range(4):
            p = prod[i * 128 : i * 128 + 128]
            h.append(diag(p[:, 0:128] + p[:, 128:256] + p[:, 256:384]))
        hbuf[z, 4 * blk : 4 * blk + 4, :] = jnp.concatenate(h, axis=0)
        return gain_sum

    gain_part = norm(1)
    pair_finish(2)
    red_forward(3)
    gain_part = gain_part + norm(0)

    def h_out(k):
        return rcopy(hbuf.at[z], hbuf.at[z], sync_ss.at[2, k], sync_rs.at[2, k], zdev(k))

    def h_in(k):
        at = hbuf.at[lax.rem(z - k + NZ, NZ)]
        return rcopy(at, at, sync_ss.at[2, k], sync_rs.at[2, k], zdev(k))

    for k in range(1, NZ):
        h_out(k).start()
    total = cl[z]
    for k in range(1, NZ):
        sync_out(k).wait_recv()
        total = total + r1[k]
    cfull[z] = total
    for k in range(1, NZ):
        sync_back(k).start()

    pair_finish(3)
    red_start(4, lambda r: xa[lax.rem(y + r, NY)])

    for k in range(1, NZ):
        h_in(k).wait_recv()
    for k in range(1, NZ):
        sync_back_in(k).wait_recv()

    proj, inv, sq, cf, wid, gw, mix_inv = coefficients()
    h8 = hbuf[0]
    for k in range(1, NZ):
        h8 = h8 + hbuf[k]
    h8 = jnp.concatenate([h8[0:4], h8[4:8]], axis=1)
    inner = sum(wid[i] * h8[i : i + 1] for i in range(4))
    kfac = mix_inv * mix_inv * mix_inv * inner / D
    rows, left = [], []
    sub8 = lax.broadcasted_iota(jnp.int32, (8, 128), 0)
    lane8 = lax.broadcasted_iota(jnp.int32, (8, 128), 1)
    stat = jnp.zeros((1, 128), F32)
    for i in range(4):
        mix_grad = mix_inv * h8[i : i + 1] - kfac * gw[i]
        route = cfull[4 + i // 2][4 * (i % 2) : 4 * (i % 2) + 4]
        cg = jnp.concatenate([cfull[i][7:8], mix_grad, route, jnp.zeros((2, T), F32)], axis=0)
        pre = cg * (1.0 - sq[i] * sq[i])
        pg = pre * inv[i]
        scale = jnp.sum(pre * proj[i], axis=0, keepdims=True) * (inv[i] * inv[i] * inv[i] / D)
        hi, mid, lo = split3(pg)
        left.append(jnp.concatenate([hi, mid, lo], axis=0))
        rows += [hi, mid, lo, wid[i], scale, cf[i][2:6], mix_inv, kfac]
        sums = jnp.broadcast_to(jnp.sum(cg, axis=1, keepdims=True), (8, 128))
        stat = stat + jnp.sum(jnp.where(lane8 == sub8 + 8 * i, sums, 0.0), axis=0, keepdims=True)
    cpart = dot_nn(jnp.concatenate(left, axis=1).astype(BF16), xs[0:4].reshape(4 * T, F))
    cpart = cpart[0:8] + cpart[8:16] + cpart[16:24]
    last = jnp.concatenate([stat, jnp.zeros((1, F - 128), F32)], axis=1)
    sb[...] = jnp.concatenate([cpart[0:6], gain_part, last], axis=0)

    sm_core = rcopy(sb, sc, sm_ss.at[0], sm_rs.at[0], cdev)
    sm_core.start()
    col2[...] = jnp.concatenate(rows, axis=0).T

    lhs = col2[...].astype(BF16)
    for i in range(4):
        acc[i] = dot_nn(lhs, cwx[i])

    def out_rows(blk, carry):
        at = pl.ds(pl.multiple_of(blk * 16, 16), 16)
        c = col2[at, :]
        mg = c[:, 30:31] * pbuf[0, at, :] - c[:, 31:32] * mixed[at, :]
        g = [gs[j, at, :].astype(F32) for j in range(4)]
        for i in range(4):
            o = 32 * i + 24
            v = acc[i, at, :] + c[:, o : o + 1] * mg - c[:, o + 1 : o + 2] * xs[i, at, :].astype(F32)
            for j in range(4):
                v = v + c[:, o + 2 + j : o + 3 + j] * g[j]
            so_v[i, at, :] = v.astype(BF16)
        return carry

    def sm_x(k):
        return rcopy(sx.at[x], sx.at[x], sm_ss.at[k], sm_rs.at[k], xdev(k))

    def sm_x_in(k):
        at = sx.at[lax.rem(x - k + NX, NX)]
        return rcopy(at, at, sm_ss.at[k], sm_rs.at[k], xdev(k))

    def sm_y(k):
        return rcopy(sy.at[y], sy.at[y], sm_ss.at[3 + k], sm_rs.at[3 + k], ydev(k))

    def sm_y_in(k):
        at = sy.at[lax.rem(y - k + NY, NY)]
        return rcopy(at, at, sm_ss.at[3 + k], sm_rs.at[3 + k], ydev(k))

    sm_core.wait_recv()
    sx[x] = sb[...] + sc[...]
    for k in (1, 2, 3):
        sm_x(k).start()
    red_forward(4)

    lax.fori_loop(0, T // 32, out_rows, 0)
    for k in (1, 2, 3):
        sm_x_in(k).wait_recv()
    sy[y] = sx[0] + sx[1] + sx[2] + sx[3]
    for k in (1, 2, 3):
        sm_y(k).start()
    lax.fori_loop(T // 32, T // 16, out_rows, 0)
    colb[...] = jnp.concatenate([cf[j][0:1] for j in range(4)] + [jnp.zeros((124, T), F32)], axis=0).T
    lax.fori_loop(0, T // 32, branch, 0)

    top, low = red_finish(4, xa[y])
    wo_v[:HB] = top
    wo_v[HB:] = low

    for k in (1, 2, 3):
        sm_y_in(k).wait_recv()
    small = sy[0] + sy[1] + sy[2] + sy[3]
    cw_o[...] = small[0:6]
    gain_o[...] = jnp.concatenate([small[6:7, i * 128 : i * 128 + 128] for i in range(F // 128)], axis=0)
    st_o[...] = jnp.concatenate([small[7:8, 8 * i : 8 * i + 6] for i in range(4)], axis=0)

    for way in (RIGHT, LEFT):
        for step in range(4):
            for half in range(2):
                if step or half == way:
                    rs_copy(way, step, half).wait_send()
        for step in range(1, 5):
            for kk in range(2):
                if step < 4 or kk == way:
                    ag_copy(way, step, kk).wait_send()
        for e in range(5):
            for part in range(3):
                red_copy(e, way, part).wait_send()
    for k in range(1, NZ):
        sync_out(k).wait_send()
        sync_back(k).wait_send()
        crit_out(k).wait_send()
        crit_back(k).wait_send()
        h_out(k).wait_send()
    q_swap.wait_send()
    for kk in range(2):
        n_swap(kk).wait_send()
    sm_core.wait_send()
    for k in (1, 2, 3):
        sm_x(k).wait_send()
        sm_y(k).wait_send()


def copy_kernel(*refs):
    src, dst, sem = refs[:6], refs[6:12], refs[12]
    copies = [pltpu.make_async_copy(src[i], dst[i], sem.at[i]) for i in range(6)]
    for c in copies:
        c.start()
    for c in copies:
        c.wait()


def local(streams, stream_grads, branch_out, query_grads, query_weight, norm_gain, coef_weight, static_coef):
    any_spec = pl.BlockSpec(memory_space=pl.ANY)
    vmem = pl.BlockSpec(memory_space=pltpu.VMEM)
    smem = pl.BlockSpec(memory_space=pltpu.SMEM)
    dma = pltpu.SemaphoreType.DMA
    outs = pl.pallas_call(
        kernel,
        out_shape=(
            pltpu.VMEM((4, T, F), BF16),
            pltpu.VMEM((T, F), BF16),
            pltpu.VMEM((RB, F), F32),
            pltpu.VMEM((F // 128, 128), F32),
            pltpu.VMEM((6, F), F32),
            pltpu.VMEM((4, 6), F32),
        ),
        in_specs=[any_spec] * 5 + [vmem, vmem, smem],
        out_specs=(vmem,) * 6,
        scratch_shapes=[
            pltpu.VMEM((5, T, F), BF16),
            pltpu.VMEM((4, T, F), BF16),
            pltpu.VMEM((2, T, F), BF16),
            pltpu.VMEM((NZ, F, F), BF16),
            pltpu.VMEM((NZ, T, F), F32),
            pltpu.VMEM((2, 4, 2, T // 2, F), BF16),
            pltpu.VMEM((2, 4, 2, T // 2, F), BF16),
            pltpu.VMEM((NZ, 8, T), F32),
            pltpu.VMEM((NZ, 8, T), F32),
            pltpu.VMEM((NZ, 8, T), F32),
            pltpu.VMEM((NZ, 2, T), F32),
            pltpu.VMEM((NZ, 2, T), F32),
            pltpu.VMEM((NZ, 2, T), F32),
            pltpu.VMEM((NZ, 8, 128), F32),
            pltpu.VMEM((T, F), F32),
            pltpu.VMEM((F, T), BF16),
            pltpu.VMEM((NZ, 2, 2, RB, T), BF16),
            pltpu.VMEM((T, 128), F32),
            pltpu.VMEM((T, 128), F32),
            pltpu.VMEM((T, 128), F32),
            pltpu.VMEM((4, 128, F), BF16),
            pltpu.VMEM((5, 2, 3, HB, F), BF16),
            pltpu.VMEM((5, 2, 3, HB, F), BF16),
            pltpu.VMEM((5, 2, HB, F), F32),
            pltpu.VMEM((NY, RB, F), F32),
            pltpu.VMEM((4, T, F), F32),
            pltpu.VMEM((8, F), F32),
            pltpu.VMEM((8, F), F32),
            pltpu.VMEM((NX, 8, F), F32),
            pltpu.VMEM((NY, 8, F), F32),
            dma((4,)),
            dma((NZ,)),
            dma((2, 4, 2)),
            dma((2, 4, 2)),
            dma((2, 5, 2)),
            dma((2, 5, 2)),
            dma((5, NZ)),
            dma((5, NZ)),
            dma((3,)),
            dma((3,)),
            dma((5, 2, 3)),
            dma((5, 2, 3)),
            dma((7,)),
            dma((7,)),
        ],
        compiler_params=pltpu.CompilerParams(
            collective_id=0, has_side_effects=True, vmem_limit_bytes=56 * 1024 * 1024
        ),
        cost_estimate=pl.CostEstimate(flops=8_000_000_000, bytes_accessed=13_000_000, transcendentals=10000),
    )(
        streams,
        stream_grads,
        branch_out,
        query_grads,
        query_weight,
        norm_gain.reshape(F // 128, 128),
        coef_weight.T,
        static_coef,
    )
    so, bo, wo, gain, cwg, stat = pl.pallas_call(
        copy_kernel,
        out_shape=[jax.ShapeDtypeStruct(o.shape, o.dtype) for o in outs],
        in_specs=[any_spec] * 6,
        out_specs=[any_spec] * 6,
        scratch_shapes=[dma((6,))],
        compiler_params=pltpu.CompilerParams(vmem_limit_bytes=1024 * 1024),
    )(*outs)
    return so, bo, wo, gain.reshape(F), cwg.T, stat


def solution(mesh):
    in_specs = (
        P(None, "dp", "tensor"),
        P(None, "dp", "tensor"),
        P("dp", "tensor"),
        P("dp", "tensor"),
        P(None, "tensor"),
        P("tensor"),
        P("tensor", None),
        P(),
    )
    out_specs = (
        P(None, "dp", "tensor"),
        P("dp", "tensor"),
        P("dp", "tensor"),
        P("tensor"),
        P("tensor", None),
        P(),
    )
    return jax.shard_map(local, mesh=mesh, in_specs=in_specs, out_specs=out_specs, check_vma=False)
```

```python
import functools

import jax
import jax.numpy as jnp
from jax import lax
from jax.experimental import pallas as pl
from jax.experimental.pallas import tpu as pltpu
from jax.sharding import PartitionSpec as P

EPS = 1e-06
MESH = pl.DeviceIdType.MESH
F32 = jnp.float32
BF16 = jnp.bfloat16

T = 256
F = 640
NZ = 8
D = F * NZ
RB = 160
HB = RB // 2
NX = 4
NY = 4


def dot_nt(a, b):
    return lax.dot_general(a, b, (((1,), (1,)), ((), ())), preferred_element_type=F32)


def dot_nn(a, b):
    return lax.dot_general(a, b, (((1,), (0,)), ((), ())), preferred_element_type=F32)


def split3(v):
    hi = v.astype(BF16).astype(F32)
    rest = v - hi
    mid = rest.astype(BF16).astype(F32)
    return hi, mid, (rest - mid).astype(BF16).astype(F32)


def kernel(
    s_h, g_h, b_h, q_h, w_h, gain, cw, st,
    so_v, bo_v, wo_v, gain_o, cw_o, st_o,
    xs, gs, qq, wbuf,
    pbuf, rs_send, rs_recv,
    cl, r1, cfull, crit, crit_r, crit_f, hbuf,
    mixed, nts, nbuf, col1, colb, col2, cwx,
    xsend, xrecv, keep, xa,
    acc, sb, sc, sx, sy,
    in_sem, win_sem,
    rs_ss, rs_rs, ag_ss, ag_rs, sync_ss, sync_rs, core_ss, core_rs, x_ss, x_rs, sm_ss, sm_rs,
):
    dp = lax.axis_index("dp")
    z = lax.axis_index("tensor")
    core = lax.rem(dp, 2)
    x = lax.rem(dp // 2, NX)
    y = dp // (2 * NX)

    def zdev(k):
        return (dp, lax.rem(z + k + NZ, NZ))

    def xdev(k):
        return ((y * NX + lax.rem(x + k + NX, NX)) * 2 + core, z)

    def ydev(k):
        return ((lax.rem(y + k + NY, NY) * NX + x) * 2 + core, z)

    cdev = (dp + 1 - 2 * core, z)

    def rcopy(src, dst, ss, rs, dev):
        return pltpu.make_async_remote_copy(
            src_ref=src, dst_ref=dst, send_sem=ss, recv_sem=rs, device_id=dev, device_id_type=MESH
        )

    gain_row = jnp.concatenate([gain[i : i + 1, :] for i in range(F // 128)], axis=1)

    q_in = pltpu.make_async_copy(q_h, qq.at[core], in_sem.at[0])
    s_in = pltpu.make_async_copy(s_h, xs.at[0:4], in_sem.at[1])
    g_in = pltpu.make_async_copy(g_h, gs, in_sem.at[2])
    b_in = pltpu.make_async_copy(b_h, xs.at[4], in_sem.at[3])

    def w_in(k):
        blk = lax.rem(z + k, NZ)
        return pltpu.make_async_copy(
            w_h.at[pl.ds(pl.multiple_of(blk * F, F), F)], wbuf.at[k], win_sem.at[k]
        )

    s_in.start()
    q_in.start()
    for k in (4, 3, 5):
        w_in(k).start()
    g_in.start()
    b_in.start()
    for k in (2, 6, 1, 7, 0):
        w_in(k).start()

    barrier = pltpu.get_barrier_semaphore()
    peers = [zdev(k) for k in range(1, NZ)] + [xdev(k) for k in (1, 2, 3)]
    peers += [ydev(k) for k in (1, 2, 3)] + [cdev]
    for dev in peers:
        pl.semaphore_signal(barrier, inc=1, device_id=dev, device_id_type=MESH)

    def rs_partial(k):
        w_in(k).wait()
        pbuf[k] = dot_nt(qq[core], wbuf[k])

    RIGHT, LEFT = 0, 1
    HALF = T // 2

    def rs_copy(way, step, half):
        return rcopy(
            rs_send.at[way, step, half],
            rs_recv.at[way, step, half],
            rs_ss.at[way, step, half],
            rs_rs.at[way, step, half],
            zdev(1 if way == RIGHT else -1),
        )

    def rs_block(way, step):
        return 4 - step if way == RIGHT else 4 + step if step else 4

    def rs_raw(way, step, half):
        rs_send[way, step, half] = pbuf[rs_block(way, step), half * HALF : (half + 1) * HALF].astype(BF16)
        rs_copy(way, step, half).start()

    def rs_add(way, step, half):
        rs_copy(way, step - 1, half).wait_recv()
        v = pbuf[rs_block(way, step), half * HALF : (half + 1) * HALF]
        rs_send[way, step, half] = (v + rs_recv[way, step - 1, half].astype(F32)).astype(BF16)
        rs_copy(way, step, half).start()

    s_in.wait()
    cw8 = jnp.concatenate([cw[...].astype(F32), jnp.zeros((10, F), F32)], axis=0).astype(BF16)
    rows_i = lax.broadcasted_iota(jnp.int32, (128, 128), 0)
    cols_i = lax.broadcasted_iota(jnp.int32, (128, 128), 1)
    eye = rows_i == cols_i

    def diag(block):
        return jnp.sum(jnp.where(eye, block, 0.0), axis=0, keepdims=True)

    def gram_s(blk, carry):
        at = pl.ds(pl.multiple_of(blk * 128, 128), 128)
        s_blk = xs[0:4, at, :].reshape(4 * 128, F)
        ss = dot_nt(s_blk, s_blk)
        gr = {
            (i, j): diag(ss[i * 128 : i * 128 + 128, j * 128 : j * 128 + 128])
            for i in range(4)
            for j in range(i, 4)
        }
        proj = dot_nt(cw8, s_blk)
        for i in range(4):
            p = proj[:, i * 128 : i * 128 + 128]
            cl[2 * i, :, at] = jnp.concatenate([p[0:1], p[2:6]], axis=0)
        off = [gr[0, 1], gr[0, 2], gr[0, 3], gr[1, 2], gr[1, 3], gr[2, 3]]
        first = [proj[1:2, i * 128 : i * 128 + 128] for i in range(4)]
        first += [gr[i, i] for i in range(4)] + off + [jnp.zeros((1, 128), F32)] * 2
        for p in range(NZ):
            crit[p, :, at] = jnp.concatenate(first[2 * p : 2 * p + 2], axis=0)
        return carry

    def gram_g(blk, carry):
        at = pl.ds(pl.multiple_of(blk * 128, 128), 128)
        sb_blk = xs[:, at, :].reshape(5 * 128, F)
        g_blk = gs[:, at, :].reshape(4 * 128, F)
        sg = dot_nt(sb_blk, g_blk)
        route = [
            [diag(sg[i * 128 : i * 128 + 128, j * 128 : j * 128 + 128]) for j in range(4)] for i in range(5)
        ]
        for i in range(4):
            cl[2 * i + 1, :, at] = jnp.concatenate([route[4][i]] + route[i], axis=0)
        return carry

    lax.fori_loop(0, 2, gram_s, 0)

    def sync_out(k):
        return rcopy(
            cl.at[lax.rem(z + k, NZ)], r1.at[k], sync_ss.at[0, k], sync_rs.at[0, k], zdev(k)
        )

    def sync_back(k):
        return rcopy(cfull.at[z], cfull.at[z], sync_ss.at[1, k], sync_rs.at[1, k], zdev(k))

    def sync_back_in(k):
        at = cfull.at[lax.rem(z - k + NZ, NZ)]
        return rcopy(at, at, sync_ss.at[1, k], sync_rs.at[1, k], zdev(k))

    def crit_out(k):
        return rcopy(
            crit.at[lax.rem(z + k, NZ)], crit_r.at[k], sync_ss.at[3, k], sync_rs.at[3, k], zdev(k)
        )

    def crit_back(k):
        return rcopy(crit_f.at[z], crit_f.at[z], sync_ss.at[4, k], sync_rs.at[4, k], zdev(k))

    def crit_back_in(k):
        at = crit_f.at[lax.rem(z - k + NZ, NZ)]
        return rcopy(at, at, sync_ss.at[4, k], sync_rs.at[4, k], zdev(k))

    q_in.wait()
    rs_partial(4)

    pl.semaphore_wait(barrier, len(peers))
    for k in range(1, NZ):
        crit_out(k).start()
    rs_raw(RIGHT, 0, 0)
    rs_raw(LEFT, 0, 1)
    q_swap = rcopy(qq.at[core], qq.at[core], core_ss.at[0], core_rs.at[0], cdev)
    q_swap.start()
    rs_partial(3)
    rs_partial(5)
    first = crit[z]
    for k in range(1, NZ):
        crit_out(k).wait_recv()
        first = first + crit_r[k]
    crit_f[z] = first
    for k in range(1, NZ):
        crit_back(k).start()
    rs_raw(RIGHT, 1, 1)
    rs_raw(LEFT, 1, 0)
    rs_partial(2)
    rs_partial(6)
    g_in.wait()
    b_in.wait()
    lax.fori_loop(0, 2, gram_g, 0)

    cw_f = cw8[0:8].astype(F32)
    for i in range(4):
        parts = [cw_f, cw_f, cw_f]
        if i:
            parts = [jnp.zeros((i * 32, F), F32)] + parts
        parts = parts + [jnp.zeros((128 - i * 32 - 24, F), F32)]
        cwx[i] = jnp.concatenate(parts, axis=0).astype(BF16)

    row8 = lax.broadcasted_iota(jnp.int32, (8, T), 0)

    def coefficients():
        proj, inv, sq, cf = [], [], [], []
        at = {(0, 1): 8, (0, 2): 9, (0, 3): 10, (1, 2): 11, (1, 3): 12, (2, 3): 13}

        def g_of(i, j):
            r = 4 + i if i == j else at[min(i, j), max(i, j)]
            return crit_f[r // 2, r % 2 : r % 2 + 1]

        for i in range(4):
            piece = cfull[2 * i]
            first = crit_f[i // 2, i % 2 : i % 2 + 1]
            p8 = jnp.concatenate([piece[0:1], first, piece[1:5], jnp.zeros((2, T), F32)], axis=0)
            iv = lax.rsqrt(g_of(i, i) / D + EPS)
            th = jnp.tanh(iv * p8)
            stc = jnp.zeros((8, T), F32)
            for c in range(6):
                stc = jnp.where(row8 == c, st[i, c], stc)
            proj.append(p8)
            inv.append(iv)
            sq.append(th)
            cf.append(stc + th)
        wid = [cf[i][1:2] for i in range(4)]
        gw = [sum(g_of(i, j) * wid[j] for j in range(4)) for i in range(4)]
        mixed_sq = sum(wid[i] * gw[i] for i in range(4))
        mix_inv = lax.rsqrt(mixed_sq / D + EPS)
        return proj, inv, sq, cf, wid, gw, mix_inv

    rs_add(RIGHT, 1, 0)
    rs_add(LEFT, 1, 1)
    for k in range(1, NZ):
        crit_back_in(k).wait_recv()

    def mix_coefficients():
        low = jnp.concatenate([crit_f[p] for p in range(4)], axis=0)
        high = jnp.concatenate([crit_f[p] for p in range(4, 7)], axis=0)
        wid = [
            st[i, 1] + jnp.tanh(lax.rsqrt(low[4 + i : 5 + i] / D + EPS) * low[i : i + 1]) for i in range(4)
        ]
        at = {(0, 1): 0, (0, 2): 1, (0, 3): 2, (1, 2): 3, (1, 3): 4, (2, 3): 5}
        mixed_sq = sum(wid[i] * wid[i] * low[4 + i : 5 + i] for i in range(4))
        mixed_sq = mixed_sq + 2.0 * sum(wid[i] * wid[j] * high[r : r + 1] for (i, j), r in at.items())
        return wid, lax.rsqrt(mixed_sq / D + EPS)

    wid, mix_inv = mix_coefficients()
    col1[...] = jnp.concatenate(wid + [mix_inv, jnp.zeros((123, T), F32)], axis=0).T

    def mix(blk, carry):
        at = pl.ds(pl.multiple_of(blk * 32, 32), 32)
        c = col1[at, :]
        m = c[:, 0:1] * xs[0, at, :].astype(F32)
        for i in range(1, 4):
            m = m + c[:, i : i + 1] * xs[i, at, :].astype(F32)
        mixed[at, :] = m
        acc[0, at, :] = m * c[:, 4:5] * gain_row
        return carry

    lax.fori_loop(0, T // 32, mix, 0)
    for lane in range(F // 128):
        tr = acc[0, :, lane * 128 : lane * 128 + 128].T.astype(BF16)
        nts[lane * 128 : lane * 128 + 128, :] = tr

    def n_swap(kk):
        return rcopy(
            nts.at[pl.ds(pl.multiple_of((2 * kk + 1 - core) * RB, 32), RB)],
            nbuf.at[z, kk, core],
            core_ss.at[1 + kk],
            core_rs.at[1 + kk],
            cdev,
        )

    def n_swap_in(kk):
        return rcopy(
            nts.at[pl.ds(pl.multiple_of((2 * kk + 1 - core) * RB, 32), RB)],
            nbuf.at[z, kk, 1 - core],
            core_ss.at[1 + kk],
            core_rs.at[1 + kk],
            cdev,
        )

    for kk in range(2):
        n_swap(kk).start()
    for kk in range(2):
        nbuf[z, kk, core] = nts[pl.ds(pl.multiple_of((2 * kk + core) * RB, 32), RB), :]

    def ag_copy(way, step, kk):
        blk = lax.rem(z - step + 1 + NZ, NZ) if way == RIGHT else lax.rem(z + step - 1, NZ)
        at = nbuf.at[blk, kk]
        return rcopy(at, at, ag_ss.at[way, step, kk], ag_rs.at[way, step, kk], zdev(1 if way == RIGHT else -1))

    def ag_in(way, step, kk):
        blk = lax.rem(z - step + NZ, NZ) if way == RIGHT else lax.rem(z + step, NZ)
        at = nbuf.at[blk, kk]
        return rcopy(at, at, ag_ss.at[way, step, kk], ag_rs.at[way, step, kk], zdev(1 if way == RIGHT else -1))

    n_swap_in(0).wait_recv()
    ag_copy(RIGHT, 1, 0).start()
    n_swap_in(1).wait_recv()
    ag_copy(LEFT, 1, 1).start()
    ag_copy(RIGHT, 1, 1).start()
    ag_copy(LEFT, 1, 0).start()

    def ag_forward(step):
        for first in range(2):
            for way in (RIGHT, LEFT):
                kk = first ^ way
                if step < 4 or kk == way:
                    ag_in(way, step - 1, kk).wait_recv()
                    ag_copy(way, step, kk).start()

    par = lax.rem(z, 2)
    z0 = z - par
    q_swap_in = rcopy(qq.at[1 - core], qq.at[1 - core], core_ss.at[0], core_rs.at[0], cdev)

    def pair_base(m):
        if m == 0:
            return z0
        if m == 3:
            return lax.rem(z0 + 4, NZ)
        sign = -1 if m == 1 else 1
        return lax.rem(z0 + sign * 2 * (1 - 2 * par) + NZ, NZ)

    def wg_block(m, r):
        xd = lax.rem(x + r, NX)
        n = nbuf.at[lax.rem(pair_base(m) + xd // 2, NZ), lax.rem(xd, 2)]
        return dot_nn(n[0], qq[0]) + dot_nn(n[1], qq[1])

    def red_copy(e, way, part):
        dev = (xdev if e < 4 else ydev)(1 if way == RIGHT else -1)
        return rcopy(
            xsend.at[e, way, part], xrecv.at[e, way, part], x_ss.at[e, way, part], x_rs.at[e, way, part], dev
        )

    def red_start(e, block):
        far = block(2).astype(BF16)
        xsend[e, RIGHT, 0] = far[:HB]
        red_copy(e, RIGHT, 0).start()
        xsend[e, LEFT, 0] = far[HB:]
        red_copy(e, LEFT, 0).start()
        near = block(1)
        xsend[e, RIGHT, 1] = near[HB:].astype(BF16)
        red_copy(e, RIGHT, 1).start()
        keep[e, RIGHT] = near[:HB]
        near = block(3)
        xsend[e, LEFT, 1] = near[:HB].astype(BF16)
        red_copy(e, LEFT, 1).start()
        keep[e, LEFT] = near[HB:]

    def red_forward(e):
        for way in (RIGHT, LEFT):
            red_copy(e, way, 0).wait_recv()
            xsend[e, way, 2] = (keep[e, way] + xrecv[e, way, 0].astype(F32)).astype(BF16)
            red_copy(e, way, 2).start()

    def red_finish(e, own):
        for way in (RIGHT, LEFT):
            for part in (1, 2):
                red_copy(e, way, part).wait_recv()
        top = own[:HB] + xrecv[e, RIGHT, 2].astype(F32) + xrecv[e, LEFT, 1].astype(F32)
        low = own[HB:] + xrecv[e, RIGHT, 1].astype(F32) + xrecv[e, LEFT, 2].astype(F32)
        return top, low

    def pair_start(m):
        red_start(m, functools.partial(wg_block, m))
        xa[pair_base(m) // 2] = wg_block(m, 0)

    def pair_finish(m):
        at = pair_base(m) // 2
        top, low = red_finish(m, xa[at])
        xa[at, :HB] = top
        xa[at, HB:] = low

    def branch(blk, carry):
        at = pl.ds(pl.multiple_of(blk * 32, 32), 32)
        c = colb[at, :]
        v = c[:, 0:1] * gs[0, at, :].astype(F32)
        for j in range(1, 4):
            v = v + c[:, j : j + 1] * gs[j, at, :].astype(F32)
        bo_v[at, :] = v.astype(BF16)
        return carry

    rs_add(RIGHT, 2, 1)
    rs_add(LEFT, 2, 0)
    for k in (1, 7, 0):
        rs_partial(k)
    q_swap_in.wait_recv()

    ag_forward(2)
    rs_add(RIGHT, 2, 0)
    rs_add(LEFT, 2, 1)
    pair_start(0)

    red_forward(0)

    ag_forward(3)
    pair_start(1)
    red_forward(1)

    ag_forward(4)
    for half in (1, 0):
        for way in (RIGHT, LEFT):
            rs_add(way, 3, half)
    for k in range(1, NZ):
        sync_out(k).start()
    ag_in(RIGHT, 3, 1).wait_recv()
    ag_in(LEFT, 3, 0).wait_recv()
    pair_start(2)
    pair_finish(0)
    red_forward(2)

    ag_in(RIGHT, 4, 0).wait_recv()
    ag_in(LEFT, 4, 1).wait_recv()
    pair_start(3)
    pair_finish(1)

    def norm(blk):
        at = slice(blk * 128, blk * 128 + 128)
        for way in (RIGHT, LEFT):
            rs_copy(way, 3, blk).wait_recv()
        ng = pbuf[0, at, :] + rs_recv[RIGHT, 3, blk].astype(F32) + rs_recv[LEFT, 3, blk].astype(F32)
        gain_sum = jnp.sum(ng * (mixed[at, :] * col1[at, 4:5]), axis=0, keepdims=True)
        scaled = ng * gain_row
        pbuf[0, at, :] = scaled
        hi, mid, lo = split3(scaled)
        parts = jnp.concatenate([hi, mid, lo], axis=0).astype(BF16)
        prod = dot_nt(xs[0:4, at, :].reshape(4 * 128, F), parts)
        h = []
        for i in range(4):
            p = prod[i * 128 : i * 128 + 128]
            h.append(diag(p[:, 0:128] + p[:, 128:256] + p[:, 256:384]))
        hbuf[z, 4 * blk : 4 * blk + 4, :] = jnp.concatenate(h, axis=0)
        return gain_sum

    gain_part = norm(1)
    pair_finish(2)
    red_forward(3)
    gain_part = gain_part + norm(0)

    def h_out(k):
        return rcopy(hbuf.at[z], hbuf.at[z], sync_ss.at[2, k], sync_rs.at[2, k], zdev(k))

    def h_in(k):
        at = hbuf.at[lax.rem(z - k + NZ, NZ)]
        return rcopy(at, at, sync_ss.at[2, k], sync_rs.at[2, k], zdev(k))

    for k in range(1, NZ):
        h_out(k).start()
    total = cl[z]
    for k in range(1, NZ):
        sync_out(k).wait_recv()
        total = total + r1[k]
    cfull[z] = total
    for k in range(1, NZ):
        sync_back(k).start()

    pair_finish(3)
    red_start(4, lambda r: xa[lax.rem(y + r, NY)])

    for k in range(1, NZ):
        h_in(k).wait_recv()
    for k in range(1, NZ):
        sync_back_in(k).wait_recv()

    proj, inv, sq, cf, wid, gw, mix_inv = coefficients()
    h8 = hbuf[0]
    for k in range(1, NZ):
        h8 = h8 + hbuf[k]
    h8 = jnp.concatenate([h8[0:4], h8[4:8]], axis=1)
    inner = sum(wid[i] * h8[i : i + 1] for i in range(4))
    kfac = mix_inv * mix_inv * mix_inv * inner / D
    rows, left = [], []
    sub8 = lax.broadcasted_iota(jnp.int32, (8, 128), 0)
    lane8 = lax.broadcasted_iota(jnp.int32, (8, 128), 1)
    stat = jnp.zeros((1, 128), F32)
    for i in range(4):
        mix_grad = mix_inv * h8[i : i + 1] - kfac * gw[i]
        own = cfull[2 * i + 1]
        cg = jnp.concatenate([own[0:1], mix_grad, own[1:5], jnp.zeros((2, T), F32)], axis=0)
        pre = cg * (1.0 - sq[i] * sq[i])
        pg = pre * inv[i]
        scale = jnp.sum(pre * proj[i], axis=0, keepdims=True) * (inv[i] * inv[i] * inv[i] / D)
        hi, mid, lo = split3(pg)
        left.append(jnp.concatenate([hi, mid, lo], axis=0))
        rows += [hi, mid, lo, wid[i], scale, cf[i][2:6], mix_inv, kfac]
        sums = jnp.broadcast_to(jnp.sum(cg, axis=1, keepdims=True), (8, 128))
        stat = stat + jnp.sum(jnp.where(lane8 == sub8 + 8 * i, sums, 0.0), axis=0, keepdims=True)
    cpart = dot_nn(jnp.concatenate(left, axis=1).astype(BF16), xs[0:4].reshape(4 * T, F))
    cpart = cpart[0:8] + cpart[8:16] + cpart[16:24]
    last = jnp.concatenate([stat, jnp.zeros((1, F - 128), F32)], axis=1)
    sb[...] = jnp.concatenate([cpart[0:6], gain_part, last], axis=0)

    sm_core = rcopy(sb, sc, sm_ss.at[0], sm_rs.at[0], cdev)
    sm_core.start()
    col2[...] = jnp.concatenate(rows, axis=0).T

    lhs = col2[...].astype(BF16)
    for i in range(4):
        acc[i] = dot_nn(lhs, cwx[i])

    def out_rows(blk, carry):
        at = pl.ds(pl.multiple_of(blk * 16, 16), 16)
        c = col2[at, :]
        mg = c[:, 30:31] * pbuf[0, at, :] - c[:, 31:32] * mixed[at, :]
        g = [gs[j, at, :].astype(F32) for j in range(4)]
        for i in range(4):
            o = 32 * i + 24
            v = acc[i, at, :] + c[:, o : o + 1] * mg - c[:, o + 1 : o + 2] * xs[i, at, :].astype(F32)
            for j in range(4):
                v = v + c[:, o + 2 + j : o + 3 + j] * g[j]
            so_v[i, at, :] = v.astype(BF16)
        return carry

    def sm_x(k):
        return rcopy(sx.at[x], sx.at[x], sm_ss.at[k], sm_rs.at[k], xdev(k))

    def sm_x_in(k):
        at = sx.at[lax.rem(x - k + NX, NX)]
        return rcopy(at, at, sm_ss.at[k], sm_rs.at[k], xdev(k))

    def sm_y(k):
        return rcopy(sy.at[y], sy.at[y], sm_ss.at[3 + k], sm_rs.at[3 + k], ydev(k))

    def sm_y_in(k):
        at = sy.at[lax.rem(y - k + NY, NY)]
        return rcopy(at, at, sm_ss.at[3 + k], sm_rs.at[3 + k], ydev(k))

    sm_core.wait_recv()
    sx[x] = sb[...] + sc[...]
    for k in (1, 2, 3):
        sm_x(k).start()
    red_forward(4)

    lax.fori_loop(0, T // 32, out_rows, 0)
    for k in (1, 2, 3):
        sm_x_in(k).wait_recv()
    sy[y] = sx[0] + sx[1] + sx[2] + sx[3]
    for k in (1, 2, 3):
        sm_y(k).start()
    lax.fori_loop(T // 32, T // 16, out_rows, 0)
    colb[...] = jnp.concatenate([cf[j][0:1] for j in range(4)] + [jnp.zeros((124, T), F32)], axis=0).T
    lax.fori_loop(0, T // 32, branch, 0)

    top, low = red_finish(4, xa[y])
    wo_v[:HB] = top
    wo_v[HB:] = low

    for k in (1, 2, 3):
        sm_y_in(k).wait_recv()
    small = sy[0] + sy[1] + sy[2] + sy[3]
    cw_o[...] = small[0:6]
    gain_o[...] = jnp.concatenate([small[6:7, i * 128 : i * 128 + 128] for i in range(F // 128)], axis=0)
    st_o[...] = jnp.concatenate([small[7:8, 8 * i : 8 * i + 6] for i in range(4)], axis=0)

    for way in (RIGHT, LEFT):
        for step in range(4):
            for half in range(2):
                if step or half == way:
                    rs_copy(way, step, half).wait_send()
        for step in range(1, 5):
            for kk in range(2):
                if step < 4 or kk == way:
                    ag_copy(way, step, kk).wait_send()
        for e in range(5):
            for part in range(3):
                red_copy(e, way, part).wait_send()
    for k in range(1, NZ):
        sync_out(k).wait_send()
        sync_back(k).wait_send()
        crit_out(k).wait_send()
        crit_back(k).wait_send()
        h_out(k).wait_send()
    q_swap.wait_send()
    for kk in range(2):
        n_swap(kk).wait_send()
    sm_core.wait_send()
    for k in (1, 2, 3):
        sm_x(k).wait_send()
        sm_y(k).wait_send()


def copy_kernel(*refs):
    src, dst, sem = refs[:6], refs[6:12], refs[12]
    copies = [pltpu.make_async_copy(src[i], dst[i], sem.at[i]) for i in range(6)]
    for c in copies:
        c.start()
    for c in copies:
        c.wait()


def local(streams, stream_grads, branch_out, query_grads, query_weight, norm_gain, coef_weight, static_coef):
    any_spec = pl.BlockSpec(memory_space=pl.ANY)
    vmem = pl.BlockSpec(memory_space=pltpu.VMEM)
    smem = pl.BlockSpec(memory_space=pltpu.SMEM)
    dma = pltpu.SemaphoreType.DMA
    outs = pl.pallas_call(
        kernel,
        out_shape=(
            pltpu.VMEM((4, T, F), BF16),
            pltpu.VMEM((T, F), BF16),
            pltpu.VMEM((RB, F), F32),
            pltpu.VMEM((F // 128, 128), F32),
            pltpu.VMEM((6, F), F32),
            pltpu.VMEM((4, 6), F32),
        ),
        in_specs=[any_spec] * 5 + [vmem, vmem, smem],
        out_specs=(vmem,) * 6,
        scratch_shapes=[
            pltpu.VMEM((5, T, F), BF16),
            pltpu.VMEM((4, T, F), BF16),
            pltpu.VMEM((2, T, F), BF16),
            pltpu.VMEM((NZ, F, F), BF16),
            pltpu.VMEM((NZ, T, F), F32),
            pltpu.VMEM((2, 4, 2, T // 2, F), BF16),
            pltpu.VMEM((2, 4, 2, T // 2, F), BF16),
            pltpu.VMEM((NZ, 5, T), F32),
            pltpu.VMEM((NZ, 5, T), F32),
            pltpu.VMEM((NZ, 5, T), F32),
            pltpu.VMEM((NZ, 2, T), F32),
            pltpu.VMEM((NZ, 2, T), F32),
            pltpu.VMEM((NZ, 2, T), F32),
            pltpu.VMEM((NZ, 8, 128), F32),
            pltpu.VMEM((T, F), F32),
            pltpu.VMEM((F, T), BF16),
            pltpu.VMEM((NZ, 2, 2, RB, T), BF16),
            pltpu.VMEM((T, 128), F32),
            pltpu.VMEM((T, 128), F32),
            pltpu.VMEM((T, 128), F32),
            pltpu.VMEM((4, 128, F), BF16),
            pltpu.VMEM((5, 2, 3, HB, F), BF16),
            pltpu.VMEM((5, 2, 3, HB, F), BF16),
            pltpu.VMEM((5, 2, HB, F), F32),
            pltpu.VMEM((NY, RB, F), F32),
            pltpu.VMEM((4, T, F), F32),
            pltpu.VMEM((8, F), F32),
            pltpu.VMEM((8, F), F32),
            pltpu.VMEM((NX, 8, F), F32),
            pltpu.VMEM((NY, 8, F), F32),
            dma((4,)),
            dma((NZ,)),
            dma((2, 4, 2)),
            dma((2, 4, 2)),
            dma((2, 5, 2)),
            dma((2, 5, 2)),
            dma((5, NZ)),
            dma((5, NZ)),
            dma((3,)),
            dma((3,)),
            dma((5, 2, 3)),
            dma((5, 2, 3)),
            dma((7,)),
            dma((7,)),
        ],
        compiler_params=pltpu.CompilerParams(
            collective_id=0, has_side_effects=True, vmem_limit_bytes=56 * 1024 * 1024
        ),
        cost_estimate=pl.CostEstimate(flops=8_000_000_000, bytes_accessed=13_000_000, transcendentals=10000),
    )(
        streams,
        stream_grads,
        branch_out,
        query_grads,
        query_weight,
        norm_gain.reshape(F // 128, 128),
        coef_weight.T,
        static_coef,
    )
    so, bo, wo, gain, cwg, stat = pl.pallas_call(
        copy_kernel,
        out_shape=[jax.ShapeDtypeStruct(o.shape, o.dtype) for o in outs],
        in_specs=[any_spec] * 6,
        out_specs=[any_spec] * 6,
        scratch_shapes=[dma((6,))],
        compiler_params=pltpu.CompilerParams(vmem_limit_bytes=1024 * 1024),
    )(*outs)
    return so, bo, wo, gain.reshape(F), cwg.T, stat


def solution(mesh):
    in_specs = (
        P(None, "dp", "tensor"),
        P(None, "dp", "tensor"),
        P("dp", "tensor"),
        P("dp", "tensor"),
        P(None, "tensor"),
        P("tensor"),
        P("tensor", None),
        P(),
    )
    out_specs = (
        P(None, "dp", "tensor"),
        P("dp", "tensor"),
        P("dp", "tensor"),
        P("tensor"),
        P("tensor", None),
        P(),
    )
    return jax.shard_map(local, mesh=mesh, in_specs=in_specs, out_specs=out_specs, check_vma=False)
```
